128 devices in a mesh: sx: 16 (over x_hi, y, core), sy: 8 (over z, x_lo).
Axes of the slice: x: 4 (x_hi: 2, x_lo: 2; x = x_hi * 2 + x_lo), y: 4, z: 4, core: 2. Of those that a mesh axis runs over, the one named last changes fastest.
Arguments:
- coeffs: float32 [2, 16, 16, 8, 128, 128], P(None, 'sx', None, 'sy'), may hold values from -6 to 6
- deform: float32 [2, 4], replicated, may hold values from -0.08 to 0.08
Outputs:
- spectrum: float32 [2, 256, 1024, 128], P(None, 'sx', 'sy')
The draws below stay inside these ranges and needn't reach their ends.
All inputs are finite; a program needn't handle non-finite values.
Results may differ from the reference program's by a relative error of at most 0.0014.
Values sent between devices are 32-bit elements; how exact they have to be, the bound alone decides.
No kernel may reach another device: no remote copies, remote signals or barrier semaphores. Data moves between devices by JAX's collectives and lax.ppermute only.
A program may use at most 64 MiB of HBM per device.

```python
import math
import jax
import jax.numpy as jnp
import numpy as np
from jax import lax

NODES = 4
MODES = 4
RHS = 8
FBX = 16
FBY = 128
SBX = 16
SBY = 8


def block_scale(own_key, shape, cuts, low, largest):
    def one(dim, shards_of):
        draws = jax.random.uniform(jax.random.fold_in(jax.random.fold_in(own_key, 6), dim), (shards_of,), jnp.float32, low / len(cuts), largest / len(cuts))
        return jnp.repeat(jnp.exp(draws), shape[dim] // shards_of).reshape((-1,) + (1,) * (len(shape) - dim - 1))

    gain = one(*cuts[0])
    for cut in cuts[1:]:
        gain = gain * one(*cut)
    return gain


def bell_draw(key, extent, width, bound, cuts=(), kind=jnp.bfloat16):
    factor_of = block_scale(key, extent, cuts, -0.22, 0.18) if cuts else 1.0
    array = jax.random.normal(key, extent, jnp.float32) * width * factor_of
    return jnp.minimum(jnp.maximum(array, -bound), bound).astype(kind)


def setup_inputs(seed: int = 0) -> dict:
    keys = jax.random.split(jax.random.key(seed), 3)
    coeffs = bell_draw(keys[0], (2, SBX, FBX, SBY, FBY, RHS * NODES * NODES), 1.0, 6.0, ((1, 16), (3, 8)), jnp.float32)
    deform = jnp.clip(jax.random.uniform(keys[1], (2, MODES), jnp.float32, -0.08, 0.08), -0.08, 0.08)
    return {"coeffs": coeffs, "deform": deform}


two_pi = 2.0 * math.pi
step_scale = math.sqrt(0.5)

def cheb_nodes(count):
    return (1.0 - np.cos(np.pi * (2.0 * np.arange(count) + 1.0) / (2.0 * count))) / 2.0

def lagrange_table(count):
    nodes = cheb_nodes(count)
    table = np.ones((count, 2, count))
    for target_row in range(count):
        for sibling in range(2):
            spots = (sibling + nodes) / 2.0
            for other_node in range(count):
                if other_node != target_row:
                    table[target_row, sibling] = table[target_row, sibling] * (spots - nodes[other_node]) / (nodes[target_row] - nodes[other_node])
    return table

def rotation(first_pos, second_pos, first_freq, second_freq, deform, scales):
    first_grid = first_pos[:, :, None, None] + jnp.zeros_like(second_pos)[None, None, :, :]
    second_grid = second_pos[None, None, :, :] + jnp.zeros_like(first_pos)[:, :, None, None]
    harmonic = jnp.arange(1, deform.shape[1] + 1).astype(jnp.float32) * math.pi
    summed = (first_grid + second_grid)[..., None] * harmonic
    differ = (first_grid - second_grid)[..., None] * harmonic
    first_warp = first_grid + lax.optimization_barrier(jnp.sum(deform[0] * jnp.sin(summed), axis=-1))
    second_warp = second_grid + lax.optimization_barrier(jnp.sum(deform[1] * jnp.sin(differ), axis=-1))
    angles = scales[0] * (first_warp[..., None, None] * first_freq[:, None]) + scales[1] * (second_warp[..., None, None] * second_freq[None, :])
    return (jnp.cos(angles), jnp.sin(angles))

def orient(own_pos, other_pos, own_centre, other_centre, along, deform, scales):
    if along == 0:
        return rotation(own_pos, other_pos, own_centre, other_centre, deform, scales)
    return rotation(other_pos, own_pos, other_centre, own_centre, deform, scales)

def advance(children, parents, along, parent_count, other_boxes, other_count, parent_freq, freq_count, other_freq, other_fcount, deform, nodes, scales):
    other_pos = (other_boxes.astype(jnp.float32)[:, None] + nodes[None, :]) / other_count
    other_centre = (other_freq.astype(jnp.float32) + 0.5) / other_fcount
    parent_pos = (parents.astype(jnp.float32)[:, None] + nodes[None, :]) / parent_count
    pattern = 'au,rkuyvfg->rkayvfg' if along == 0 else 'bv,rxukvfg->rxukbfg'
    pieces = []
    for freq_child in range(2):
        centre = ((2 * parent_freq + freq_child).astype(jnp.float32) + 0.5) / (2 * freq_count)
        total_real = None
        total_imag = None
        for member, boxes, weights in children:
            child_pos = (boxes.astype(jnp.float32)[:, None] + nodes[None, :]) / (2 * parent_count)
            cosine, sine = orient(child_pos, other_pos, centre, other_centre, along, deform, scales)
            real_part = member[0] * cosine + member[1] * sine
            imag_part = member[1] * cosine - member[0] * sine
            mixed_real = jnp.einsum(pattern, weights, real_part, precision=lax.Precision.HIGHEST)
            mixed_imag = jnp.einsum(pattern, weights, imag_part, precision=lax.Precision.HIGHEST)
            if total_real is None:
                total_real, total_imag = (mixed_real, mixed_imag)
            else:
                total_real, total_imag = (total_real + mixed_real, total_imag + mixed_imag)
        cosine, sine = orient(parent_pos, other_pos, centre, other_centre, along, deform, scales)
        out_real = (total_real * cosine - total_imag * sine) * step_scale
        out_imag = (total_imag * cosine + total_real * sine) * step_scale
        pieces.append(jnp.stack([out_real, out_imag], axis=0))
    if along == 0:
        joined = jnp.stack(pieces, axis=7)
        dims = joined.shape
        return joined.reshape(dims[:6] + (dims[6] * 2, dims[8]))
    joined = jnp.stack(pieces, axis=8)
    dims = joined.shape
    return joined.reshape(dims[:7] + (dims[7] * 2,))

def local_levels(state, x_boxes, y_boxes, x_freq, x_count, y_freq, y_count, deform, nodes, lagrange, scales):
    x_bits = x_boxes.shape[0].bit_length() - 1
    y_bits = y_boxes.shape[0].bit_length() - 1
    pair_idx = jnp.arange(2).astype(jnp.int32)
    for depth in range(max(x_bits, y_bits)):
        if depth < x_bits:
            pairs = x_boxes.shape[0] // 2
            dims = state.shape
            split = state.reshape(dims[0], dims[1], pairs, 2, dims[3], dims[4], dims[5], dims[6], dims[7])
            parent_boxes = jnp.arange(pairs).astype(jnp.int32)
            children = [(split[:, :, :, 0], 2 * parent_boxes, lagrange[:, 0]), (split[:, :, :, 1], 2 * parent_boxes + 1, lagrange[:, 1])]
            state = advance(children, parent_boxes, 0, pairs, y_boxes, y_boxes.shape[0], x_freq, x_count, y_freq, y_count, deform, nodes, scales)
            x_freq = (2 * x_freq[:, None] + pair_idx[None, :]).reshape(-1)
            x_count = 2 * x_count
            x_boxes = parent_boxes
        if depth < y_bits:
            pairs = y_boxes.shape[0] // 2
            dims = state.shape
            split = state.reshape(dims[0], dims[1], dims[2], dims[3], pairs, 2, dims[5], dims[6], dims[7])
            parent_boxes = jnp.arange(pairs).astype(jnp.int32)
            children = [(split[:, :, :, :, :, 0], 2 * parent_boxes, lagrange[:, 0]), (split[:, :, :, :, :, 1], 2 * parent_boxes + 1, lagrange[:, 1])]
            state = advance(children, parent_boxes, 1, pairs, x_boxes, x_boxes.shape[0], y_freq, y_count, x_freq, x_count, deform, nodes, scales)
            y_freq = (2 * y_freq[:, None] + pair_idx[None, :]).reshape(-1)
            y_count = 2 * y_count
            y_boxes = parent_boxes
    return state

def reference(coeffs, deform):
    node_count = NODES
    right_sides = RHS
    space_x = coeffs.shape[1]
    freq_x = coeffs.shape[2]
    space_y = coeffs.shape[3]
    freq_y = coeffs.shape[4]
    old = coeffs.reshape(2, space_x, freq_x, space_y, freq_y, right_sides, node_count, node_count)
    old = jnp.transpose(old, (0, 5, 1, 6, 3, 7, 2, 4))
    nodes = jnp.asarray(cheb_nodes(node_count), dtype=jnp.float32)
    lagrange = jnp.asarray(lagrange_table(node_count), dtype=jnp.float32)
    scales = (two_pi * float(space_x * freq_x), two_pi * float(space_y * freq_y))

    def single(column):
        state = column[:, None]
        x_boxes = jnp.arange(space_x).astype(jnp.int32)
        y_boxes = jnp.arange(space_y).astype(jnp.int32)
        x_freq = jnp.arange(freq_x).astype(jnp.int32)
        y_freq = jnp.arange(freq_y).astype(jnp.int32)
        final = local_levels(state, x_boxes, y_boxes, x_freq, freq_x, y_freq, freq_y, deform, nodes, lagrange, scales)
        return final[:, 0, 0, :, 0, :, :, :]
    result = lax.map(single, jnp.moveaxis(old, 1, 0))
    result = jnp.moveaxis(result, 0, 1)
    result = jnp.transpose(result, (0, 4, 5, 1, 2, 3))
    dims = result.shape
    return result.reshape(2, dims[1], dims[2], right_sides * node_count * node_count)
```

```python
import math

import jax
import jax.numpy as jnp
import numpy as np
from jax import lax
from jax.experimental import pallas as pl
from jax.experimental.pallas import tpu as pltpu
from jax.sharding import PartitionSpec as P

NODES = 4
RHS = 8
POINTS = NODES * NODES
LANES = RHS * POINTS
MIB = 1 << 20


def cheb_nodes(count):
    return (1.0 - np.cos(np.pi * (2.0 * np.arange(count) + 1.0) / (2.0 * count))) / 2.0


def lagrange_table(count):
    nodes = cheb_nodes(count)
    table = np.ones((count, 2, count))
    for row in range(count):
        for sibling in range(2):
            spots = (sibling + nodes) / 2.0
            for other in range(count):
                if other != row:
                    table[row, sibling] *= (spots - nodes[other]) / (nodes[row] - nodes[other])
    return table


def pattern_x():
    L, e2, e4, one = lagrange_table(NODES), np.eye(2), np.eye(NODES), np.ones((2, 2))
    return np.einsum("hH,yY,zZ,asu,vV->hyzavHsYZuV", e2, e2, one, L, e4).reshape(128, 256)


def pattern_y():
    L, e2, e4, one = lagrange_table(NODES), np.eye(2), np.eye(NODES), np.ones((2, 2))
    return np.einsum("hH,zZ,aA,bsv->hzabHsZAv", e2, one, e4, L).reshape(64, 128)


def pattern_x_last():
    L, e4, one = lagrange_table(NODES), np.eye(NODES), np.ones((2, 2))
    return np.einsum("zZ,asu,bB->zabsZuB", one, L, e4).reshape(32, 64)


def pattern_y_first():
    L, e2, e4, one = lagrange_table(NODES), np.eye(2), np.eye(NODES), np.ones((2, 2))
    return np.einsum("gG,hH,zZ,uU,bsv->ghzubGHsZUv", e4, e2, one, e4, L).reshape(256, 512)


def columns(dims, first, second, first_turns, second_turns):
    names, sizes = zip(*dims)
    grid = dict(zip(names, np.meshgrid(*[np.arange(s) for s in sizes], indexing="ij")))
    shape = grid["z"].shape
    flat = lambda v: np.broadcast_to(v, shape).reshape(-1)
    return np.stack(
        [flat(first(grid)), flat(second(grid)), flat(first_turns), flat(second_turns), flat(grid["z"])]
    )


def column_tables():
    q = cheb_nodes(NODES)
    groups = []
    for gx in range(4):
        for gy in range(4):
            one = columns(
                [("h", 2), ("l", 2), ("y", 2), ("z", 2), ("u", 4), ("v", 4)],
                lambda g: (4 * gx + 2 * g["h"] + g["l"] + q[g["u"]]) / 16,
                lambda g: (2 * gy + g["y"] + q[g["v"]]) / 8,
                4.0,
                0.0,
            )
            two = columns(
                [("h", 2), ("y", 2), ("z", 2), ("u", 4), ("v", 4)],
                lambda g: (2 * gx + g["h"] + q[g["u"]]) / 8,
                lambda g: (2 * gy + g["y"] + q[g["v"]]) / 8,
                0.0,
                2.0,
            )
            three = columns(
                [("h", 2), ("z", 2), ("u", 4), ("v", 4)],
                lambda g: (2 * gx + g["h"] + q[g["u"]]) / 8,
                lambda g: (gy + q[g["v"]]) / 4,
                2.0,
                0.0,
            )
            groups.append(np.concatenate([one, two, three, np.zeros((5, 64))], axis=1))
    inner = np.stack(groups, axis=1)
    four = columns(
        [("g", 4), ("h", 2), ("l", 2), ("z", 2), ("u", 4), ("v", 4)],
        lambda g: (g["g"] + q[g["u"]]) / 4,
        lambda g: (2 * g["h"] + g["l"] + q[g["v"]]) / 4,
        0.0,
        1.0,
    )
    five = columns(
        [("h", 2), ("l", 2), ("y", 2), ("z", 2), ("u", 4), ("v", 4)],
        lambda g: (2 * g["h"] + g["l"] + q[g["u"]]) / 4,
        lambda g: (g["y"] + q[g["v"]]) / 2,
        1.0,
        0.0,
    )
    six = columns(
        [("h", 2), ("y", 2), ("z", 2), ("u", 4), ("v", 4)],
        lambda g: (g["h"] + q[g["u"]]) / 2,
        lambda g: (g["y"] + q[g["v"]]) / 2,
        0.0,
        0.5,
    )
    seven = columns(
        [("h", 2), ("z", 2), ("u", 4), ("v", 4)],
        lambda g: (g["h"] + q[g["u"]]) / 2,
        lambda g: q[g["v"]] + 0.0 * g["h"],
        0.5,
        0.0,
    )
    outer = np.concatenate([four, five, six, seven, np.zeros((5, 64))], axis=1)
    outer = np.broadcast_to(outer[:, None], (5, 8, 1024))
    return inner.astype(np.float32), outer.astype(np.float32)


def lane_nodes():
    lane = np.arange(LANES)
    q = cheb_nodes(NODES)
    both = np.stack([q[lane // NODES % NODES], q[lane % NODES]])
    return np.broadcast_to(both[:, None], (2, 8, LANES)).astype(np.float32)


SINE = [
    (-1) ** k * (2.0 * math.pi) ** (2 * k + 1) / math.factorial(2 * k + 1) for k in range(7)
]


def sine_quarter(x):
    square = x * x
    total = jnp.full_like(x, SINE[-1])
    for coefficient in SINE[-2::-1]:
        total = total * square + coefficient
    return total * x


def turn(x):
    part = x - jnp.round(x)
    size = jnp.abs(part)
    folded = jnp.where(size > 0.25, jnp.where(part > 0, 0.5, -0.5) - part, part)
    return sine_quarter(0.25 - size), sine_quarter(folded)


def sine(x):
    part = x - jnp.round(x)
    folded = jnp.where(jnp.abs(part) > 0.25, jnp.where(part > 0, 0.5, -0.5) - part, part)
    return sine_quarter(folded)


def warp(deform, first, second):
    total, differ = 0.5 * (first + second), 0.5 * (first - second)
    y1, y2 = None, None
    for m in range(4):
        one = deform[0, m] * sine(total * (m + 1.0))
        two = deform[1, m] * sine(differ * (m + 1.0))
        y1 = one if y1 is None else y1 + one
        y2 = two if y2 is None else y2 + two
    return first + y1, second + y2


def exchange(values, lane):
    width = values[0].shape[-1]
    for bit in range(3):
        step = 1 << bit
        low = (lane & step) == 0
        new = list(values)
        for i in range(8):
            if not i & step:
                a, b = values[i], values[i | step]
                new[i] = jnp.where(low, a, pltpu.roll(b, step, 1))
                new[i | step] = jnp.where(low, pltpu.roll(a, width - step, 1), b)
        values = new
    return values


def split(x):
    high = x.astype(jnp.bfloat16)
    low = (x - high.astype(jnp.float32)).astype(jnp.bfloat16)
    return high, low


def iota(shape, dim):
    return lax.broadcasted_iota(jnp.int32, shape, dim)


PRE_BOXES = 4


def pre_kernel(deform, nodes, coeffs, out, first_cos, first_sin, second_cos, second_sin):
    step = pl.program_id(0)

    @pl.when(step == 0)
    def _():
        sx = lax.axis_index("sx").astype(jnp.float32)
        sy = lax.axis_index("sy").astype(jnp.float32)
        y1, y2 = warp(deform, (nodes[0] + sx) * (1 / 16), (nodes[1] + sy) * (1 / 8))
        y1, y2 = y1[0:1] * 16.0, y2[0:1] * 8.0
        box = iota((16, LANES), 0).astype(jnp.float32) + 0.5
        c, s = turn(y1 * box)
        first_cos[...] = c
        first_sin[...] = s
        row = iota((128, LANES), 0)
        box = ((row & 7) * 16 + (row >> 3)).astype(jnp.float32) + 0.5
        c, s = turn(y2 * box)
        second_cos[...] = c
        second_sin[...] = s

    lane = iota((16, LANES), 1)

    def one(j, carry):
        b1 = step * PRE_BOXES + j
        c1, s1 = first_cos[pl.ds(b1, 1), :], first_sin[pl.ds(b1, 1), :]
        c2, s2 = second_cos[...], second_sin[...]
        c = c1 * c2 - s1 * s2
        s = s1 * c2 + c1 * s2
        both = [
            jnp.concatenate(
                [coeffs[z, 0, j, 0, pl.ds(f, 8, stride=16), :] for f in range(16)], axis=0
            )
            for z in range(2)
        ]
        rotated = (both[0] * c + both[1] * s, both[1] * c - both[0] * s)
        for z in range(2):
            flipped = rotated[z].T
            pieces = exchange([flipped[16 * r : 16 * r + 16] for r in range(8)], lane)
            for k in range(8):
                out[j * 8 + k, pl.ds(16 * z, 16), :] = pieces[k]
        return carry

    lax.fori_loop(0, PRE_BOXES, one, 0)


def pre(coeffs, deform):
    smem = pl.BlockSpec(memory_space=pltpu.SMEM)
    return pl.pallas_call(
        pre_kernel,
        grid=(16 // PRE_BOXES,),
        out_shape=jax.ShapeDtypeStruct((128, 32, 128), jnp.float32),
        in_specs=[
            smem,
            pl.BlockSpec((2, 8, LANES), lambda i: (0, 0, 0)),
            pl.BlockSpec((2, 1, PRE_BOXES, 1, 128, LANES), lambda i: (0, 0, i, 0, 0, 0)),
        ],
        out_specs=pl.BlockSpec((8 * PRE_BOXES, 32, LANES), lambda i: (i, 0, 0)),
        scratch_shapes=[
            pltpu.VMEM((16, LANES), jnp.float32),
            pltpu.VMEM((16, LANES), jnp.float32),
            pltpu.VMEM((128, LANES), jnp.float32),
            pltpu.VMEM((128, LANES), jnp.float32),
        ],
        cost_estimate=pl.CostEstimate(
            flops=10 * MIB, bytes_accessed=4 * MIB, transcendentals=0
        ),
    )(deform, jnp.asarray(lane_nodes()), coeffs)


def phase_rows(tables, deform, store):
    y1, y2 = warp(deform, tables[0], tables[1])
    c, s = turn(tables[2] * y1 + tables[3] * y2)
    real = tables[4] < 0.5
    for child in range(2):
        sine_part = s if child else -s
        store[child, 0] = jnp.where(real, c, sine_part)
        store[child, 1] = jnp.where(real, -sine_part, c)


def dot(a, b):
    return jnp.dot(a, b, precision=lax.Precision.HIGHEST, preferred_element_type=jnp.float32)


def level(pattern, rows, child, part):
    shape = pattern.shape
    real = (iota(shape, 0) & POINTS) == 0
    return pattern * jnp.where(real, rows[child][0][:, part], rows[child][1][:, part])


def build_kernel(
    deform, nodes, inner, outer, wide, px, py, px_last, m1, m2, first, second, rows_in, rows_out
):
    phase_rows(inner, deform, rows_in)
    phase_rows(outer, deform, rows_out)

    def chain(rows, at_x, at_y, at_last):
        last = jnp.concatenate(
            [level(px_last[...], rows, c, slice(at_last, at_last + 64)) for c in range(2)], axis=0
        )
        parts = [dot(last, level(py[...], rows, c, slice(at_y, at_y + 128))) for c in range(2)]
        joined = jnp.concatenate(
            [parts[cy][32 * cx : 32 * cx + 32] for cx in range(2) for cy in range(2)], axis=0
        )
        return [
            dot(joined, level(px[...], rows, c, slice(at_x, at_x + 256))) for c in range(2)
        ]

    def group(g, carry):
        rows = [[rows_in[c, z, pl.ds(g, 1), :] for z in range(2)] for c in range(2)]
        for c, value in enumerate(chain(rows, 0, 256, 384)):
            high, low = split(value)
            m1[g, pl.ds(128 * c, 128), :] = high
            m1[g, pl.ds(256 + 128 * c, 128), :] = low
        return carry

    lax.fori_loop(0, 16, group, 0)

    rows = [[rows_out[c, z, 0:1, :] for z in range(2)] for c in range(2)]
    for c5, value in enumerate(chain(rows, 512, 768, 896)):
        for c4 in range(2):
            block = dot(value, level(wide[...], rows, c4, slice(0, 512)))
            for c7 in range(2):
                for c6 in range(2):
                    high, low = split(block[64 * c7 + 32 * c6 : 64 * c7 + 32 * c6 + 32])
                    at = 32 * (8 * c5 + 4 * c7 + 2 * c4 + c6)
                    m2[0, pl.ds(at, 32), :] = high
                    m2[1, pl.ds(at, 32), :] = low

    sx = lax.axis_index("sx").astype(jnp.float32)
    sy = lax.axis_index("sy").astype(jnp.float32)
    y1, y2 = warp(deform, nodes[0], nodes[1])
    c, s = turn(y1[0:1] * (iota((16, LANES), 0).astype(jnp.float32) + (16.0 * sx + 0.5)))
    scale = math.sqrt(0.5) ** 7
    first[0] = c * scale
    first[1] = s * scale
    c, s = turn(y2[0:1] * (iota((128, LANES), 0).astype(jnp.float32) + (128.0 * sy + 0.5)))
    second[0] = c
    second[1] = s


def build(deform):
    inner, outer = column_tables()
    consts = [lane_nodes(), inner, outer, pattern_y_first(), pattern_x(), pattern_y(), pattern_x_last()]
    vmem = pl.BlockSpec(memory_space=pltpu.VMEM)
    return pl.pallas_call(
        build_kernel,
        out_shape=[
            jax.ShapeDtypeStruct((16, 512, 256), jnp.bfloat16),
            jax.ShapeDtypeStruct((2, 512, 512), jnp.bfloat16),
            jax.ShapeDtypeStruct((2, 16, LANES), jnp.float32),
            jax.ShapeDtypeStruct((2, 128, LANES), jnp.float32),
        ],
        in_specs=[pl.BlockSpec(memory_space=pltpu.SMEM)] + [vmem] * 7,
        out_specs=[vmem] * 4,
        scratch_shapes=[
            pltpu.VMEM((2, 2, 16, 512), jnp.float32),
            pltpu.VMEM((2, 2, 8, 1024), jnp.float32),
        ],
        compiler_params=pltpu.CompilerParams(vmem_limit_bytes=32 * MIB),
        cost_estimate=pl.CostEstimate(
            flops=6000 * MIB, bytes_accessed=40 * MIB, transcendentals=0
        ),
    )(deform, *[jnp.asarray(c, dtype=jnp.float32) for c in consts])


def mul(a, b):
    return jnp.dot(a, b, preferred_element_type=jnp.float32)


def post_kernel(m1, m2, first, second, got, out, high, low, acc, done, sems):
    def stage_one(g, carry):
        gx, gy = g // 4, g % 4
        x = jnp.concatenate(
            [got[pl.ds((4 * gx + i) * 8 + 2 * gy, 2)].reshape(64, LANES) for i in range(4)], axis=0
        )
        xh, xl = split(x)
        res = mul(m1[g], jnp.concatenate([xh, xl], axis=1))
        res = res[:256, :128] + (res[:256, 128:] + res[256:, :128])
        yh, yl = split(res)
        for c13 in range(4):
            for c2 in range(2):
                piece = slice(64 * c13 + 32 * c2, 64 * c13 + 32 * c2 + 32)
                at = pl.ds(pl.multiple_of(32 * g, 32), 32)
                high[c13, at, pl.ds(128 * c2, 128)] = yh[piece]
                low[c13, at, pl.ds(128 * c2, 128)] = yl[piece]
        return carry

    lax.fori_loop(0, 16, stage_one, 0)

    lane = iota((16, LANES), 1)

    def copies(c13):
        return [
            pltpu.make_async_copy(
                done.at[z, pl.ds(4 * c13, 4)], out.at[z, pl.ds(4 * c13, 4)], sems.at[z, c13]
            )
            for z in range(2)
        ]

    for c13 in range(4):
        acc[...] = mul(m2[0], high[c13]) + (mul(m2[0], low[c13]) + mul(m2[1], high[c13]))

        def finish(c57, carry):
            cx = 4 * c13 + c57
            c1, s1 = first[0, pl.ds(cx, 1), :], first[1, pl.ds(cx, 1), :]
            c2, s2 = second[0], second[1]
            c = c1 * c2 - s1 * s2
            s = s1 * c2 + c1 * s2
            turned = []
            for z in range(2):
                pieces = []
                for cy in range(8):
                    top, rest = cy >> 2, cy & 3
                    at = pl.multiple_of(128 * c57, 128) + 32 * rest + 16 * z
                    pieces.append(acc[pl.ds(at, 16), pl.ds(128 * top, 128)])
                turned.append(jnp.concatenate(exchange(pieces, lane), axis=0).T)
            done[0, cx] = turned[0] * c - turned[1] * s
            done[1, cx] = turned[1] * c + turned[0] * s
            return carry

        lax.fori_loop(0, 4, finish, 0)
        for copy in copies(c13):
            copy.start()
    for c13 in range(4):
        for copy in copies(c13):
            copy.wait()


def post(m1, m2, first, second, got):
    vmem = pl.BlockSpec(memory_space=pltpu.VMEM)
    return pl.pallas_call(
        post_kernel,
        out_shape=jax.ShapeDtypeStruct((2, 16, 128, LANES), jnp.float32),
        in_specs=[vmem] * 5,
        out_specs=pl.BlockSpec(memory_space=pl.ANY),
        scratch_shapes=[
            pltpu.VMEM((4, 512, 256), jnp.bfloat16),
            pltpu.VMEM((4, 512, 256), jnp.bfloat16),
            pltpu.VMEM((512, 256), jnp.float32),
            pltpu.VMEM((2, 16, 128, LANES), jnp.float32),
            pltpu.SemaphoreType.DMA((2, 4)),
        ],
        compiler_params=pltpu.CompilerParams(vmem_limit_bytes=32 * MIB),
        cost_estimate=pl.CostEstimate(
            flops=4000 * MIB, bytes_accessed=10 * MIB, transcendentals=0
        ),
    )(m1, m2, first, second, got)


def body(coeffs, deform):
    sent = pre(coeffs, deform)
    got = lax.all_to_all(sent, ("sx", "sy"), 0, 0, tiled=True)
    return post(*build(deform), got)


def solution(mesh):
    placed = (P(None, "sx", None, "sy", None, None), P())
    return jax.shard_map(
        body, mesh=mesh, in_specs=placed, out_specs=P(None, "sx", "sy", None), check_vma=False
    )
```

```python
import math

import jax
import jax.numpy as jnp
import numpy as np
from jax import lax
from jax.experimental import pallas as pl
from jax.experimental.pallas import tpu as pltpu
from jax.sharding import PartitionSpec as P

NODES = 4
RHS = 8
POINTS = NODES * NODES
LANES = RHS * POINTS
MIB = 1 << 20


def cheb_nodes(count):
    return (1.0 - np.cos(np.pi * (2.0 * np.arange(count) + 1.0) / (2.0 * count))) / 2.0


def lagrange_table(count):
    nodes = cheb_nodes(count)
    table = np.ones((count, 2, count))
    for row in range(count):
        for sibling in range(2):
            spots = (sibling + nodes) / 2.0
            for other in range(count):
                if other != row:
                    table[row, sibling] *= (spots - nodes[other]) / (nodes[row] - nodes[other])
    return table


def pattern_x():
    L, e2, e4, one = lagrange_table(NODES), np.eye(2), np.eye(NODES), np.ones((2, 2))
    return np.einsum("hH,yY,zZ,asu,vV->hyzavHsYZuV", e2, e2, one, L, e4).reshape(128, 256)


def pattern_y():
    L, e2, e4, one = lagrange_table(NODES), np.eye(2), np.eye(NODES), np.ones((2, 2))
    return np.einsum("hH,zZ,aA,bsv->hzabHsZAv", e2, one, e4, L).reshape(64, 128)


def pattern_x_last():
    L, e4, one = lagrange_table(NODES), np.eye(NODES), np.ones((2, 2))
    return np.einsum("zZ,asu,bB->zabsZuB", one, L, e4).reshape(32, 64)


def pattern_y_first():
    L, e2, e4, one = lagrange_table(NODES), np.eye(2), np.eye(NODES), np.ones((2, 2))
    return np.einsum("gG,hH,zZ,uU,bsv->ghzubGHsZUv", e4, e2, one, e4, L).reshape(256, 512)


def columns(dims, first, second, first_turns, second_turns):
    names, sizes = zip(*dims)
    grid = dict(zip(names, np.meshgrid(*[np.arange(s) for s in sizes], indexing="ij")))
    shape = grid["z"].shape
    flat = lambda v: np.broadcast_to(v, shape).reshape(-1)
    return np.stack(
        [flat(first(grid)), flat(second(grid)), flat(first_turns), flat(second_turns), flat(grid["z"])]
    )


def column_tables():
    q = cheb_nodes(NODES)
    groups = []
    for gx in range(4):
        for gy in range(4):
            one = columns(
                [("h", 2), ("l", 2), ("y", 2), ("z", 2), ("u", 4), ("v", 4)],
                lambda g: (4 * gx + 2 * g["h"] + g["l"] + q[g["u"]]) / 16,
                lambda g: (2 * gy + g["y"] + q[g["v"]]) / 8,
                4.0,
                0.0,
            )
            two = columns(
                [("h", 2), ("y", 2), ("z", 2), ("u", 4), ("v", 4)],
                lambda g: (2 * gx + g["h"] + q[g["u"]]) / 8,
                lambda g: (2 * gy + g["y"] + q[g["v"]]) / 8,
                0.0,
                2.0,
            )
            three = columns(
                [("h", 2), ("z", 2), ("u", 4), ("v", 4)],
                lambda g: (2 * gx + g["h"] + q[g["u"]]) / 8,
                lambda g: (gy + q[g["v"]]) / 4,
                2.0,
                0.0,
            )
            groups.append(np.concatenate([one, two, three, np.zeros((5, 64))], axis=1))
    inner = np.stack(groups, axis=1)
    four = columns(
        [("g", 4), ("h", 2), ("l", 2), ("z", 2), ("u", 4), ("v", 4)],
        lambda g: (g["g"] + q[g["u"]]) / 4,
        lambda g: (2 * g["h"] + g["l"] + q[g["v"]]) / 4,
        0.0,
        1.0,
    )
    five = columns(
        [("h", 2), ("l", 2), ("y", 2), ("z", 2), ("u", 4), ("v", 4)],
        lambda g: (2 * g["h"] + g["l"] + q[g["u"]]) / 4,
        lambda g: (g["y"] + q[g["v"]]) / 2,
        1.0,
        0.0,
    )
    six = columns(
        [("h", 2), ("y", 2), ("z", 2), ("u", 4), ("v", 4)],
        lambda g: (g["h"] + q[g["u"]]) / 2,
        lambda g: (g["y"] + q[g["v"]]) / 2,
        0.0,
        0.5,
    )
    seven = columns(
        [("h", 2), ("z", 2), ("u", 4), ("v", 4)],
        lambda g: (g["h"] + q[g["u"]]) / 2,
        lambda g: q[g["v"]] + 0.0 * g["h"],
        0.5,
        0.0,
    )
    outer = np.concatenate([four, five, six, seven, np.zeros((5, 64))], axis=1)
    outer = np.broadcast_to(outer[:, None], (5, 8, 1024))
    return inner.astype(np.float32), outer.astype(np.float32)


SINE = [
    (-1) ** k * (2.0 * math.pi) ** (2 * k + 1) / math.factorial(2 * k + 1) for k in range(7)
]


def sine_quarter(x):
    square = x * x
    total = jnp.full_like(x, SINE[-1])
    for coefficient in SINE[-2::-1]:
        total = total * square + coefficient
    return total * x


def turn(x):
    part = x - jnp.round(x)
    size = jnp.abs(part)
    folded = jnp.where(size > 0.25, jnp.where(part > 0, 0.5, -0.5) - part, part)
    return sine_quarter(0.25 - size), sine_quarter(folded)


def sine(x):
    part = x - jnp.round(x)
    folded = jnp.where(jnp.abs(part) > 0.25, jnp.where(part > 0, 0.5, -0.5) - part, part)
    return sine_quarter(folded)


def warp(deform, first, second):
    total, differ = 0.5 * (first + second), 0.5 * (first - second)
    y1, y2 = None, None
    for m in range(4):
        one = deform[0, m] * sine(total * (m + 1.0))
        two = deform[1, m] * sine(differ * (m + 1.0))
        y1 = one if y1 is None else y1 + one
        y2 = two if y2 is None else y2 + two
    return first + y1, second + y2


def flip_maps():
    row, lane = iota((8, LANES), 0), iota((8, LANES), 1)
    spot = lane & 15
    back, on = row - spot, row + spot
    lanes = [(lane & ~15) | ((back + 8 * half) & 15) for half in range(2)]
    return back & 7, (back & 8) == 0, lanes, on & 7, (on & 8) == 0


def flip(low, high, maps):
    rows, first, lanes, rows_back, first_back = maps

    def spread(x, y, rows, first):
        x = jnp.take_along_axis(x, rows, axis=0)
        y = jnp.take_along_axis(y, rows, axis=0)
        return jnp.where(first, x, y), jnp.where(first, y, x)

    low, high = spread(low, high, rows, first)
    low = jnp.take_along_axis(low, lanes[0], axis=1)
    high = jnp.take_along_axis(high, lanes[1], axis=1)
    return spread(low, high, rows_back, first_back)


def split(x):
    high = x.astype(jnp.bfloat16)
    low = (x - high.astype(jnp.float32)).astype(jnp.bfloat16)
    return high, low


def lane_nodes():
    lane = iota((8, LANES), 1)
    q = [float(v) for v in cheb_nodes(NODES)]

    def pick(t):
        return jnp.where(t < 2, jnp.where(t == 0, q[0], q[1]), jnp.where(t == 2, q[2], q[3]))

    return pick((lane >> 2) & 3), pick(lane & 3)


def iota(shape, dim):
    return lax.broadcasted_iota(jnp.int32, shape, dim)


PARTS = 4
BOXES = 16 // PARTS


def pre_kernel(deform, coeffs, out, held, ready, first_cos, first_sin, second_cos, second_sin, sems, out_sems):
    copies = [
        pltpu.make_async_copy(
            coeffs.at[:, 0, pl.ds(BOXES * p, BOXES), 0], held.at[:, pl.ds(BOXES * p, BOXES)], sems.at[p]
        )
        for p in range(PARTS)
    ]
    sends = [
        pltpu.make_async_copy(
            ready.at[pl.ds(8 * BOXES * p, 8 * BOXES)], out.at[pl.ds(8 * BOXES * p, 8 * BOXES)], out_sems.at[p]
        )
        for p in range(PARTS)
    ]
    for copy in copies:
        copy.start()

    nodes = lane_nodes()
    sx = lax.axis_index("sx").astype(jnp.float32)
    sy = lax.axis_index("sy").astype(jnp.float32)
    y1, y2 = warp(deform, (nodes[0] + sx) * (1 / 16), (nodes[1] + sy) * (1 / 8))
    y1, y2 = y1[0:1] * 16.0, y2[0:1] * 8.0
    first_cos[...], first_sin[...] = turn(y1 * (iota((16, LANES), 0).astype(jnp.float32) + 0.5))
    second_cos[...], second_sin[...] = turn(y2 * (iota((128, LANES), 0).astype(jnp.float32) + 0.5))
    maps = flip_maps()

    def one(b1, carry):
        c1, s1 = first_cos[pl.ds(b1, 1), :], first_sin[pl.ds(b1, 1), :]
        for k in range(8):
            turned = []
            for half in range(2):
                at = pl.ds(16 * k + 8 * half, 8)
                c2, s2 = second_cos[at, :], second_sin[at, :]
                c = c1 * c2 - s1 * s2
                s = s1 * c2 + c1 * s2
                re, im = held[0, b1, at, :], held[1, b1, at, :]
                turned.append((re * c + im * s, im * c - re * s))
            for z in range(2):
                low, high = flip(turned[0][z], turned[1][z], maps)
                ready[b1 * 8 + k, pl.ds(16 * z, 8), :] = low
                ready[b1 * 8 + k, pl.ds(16 * z + 8, 8), :] = high
        return carry

    for p in range(PARTS):
        copies[p].wait()
        lax.fori_loop(BOXES * p, BOXES * (p + 1), one, 0, unroll=2)
        sends[p].start()
    for send in sends:
        send.wait()


def pre(coeffs, deform):
    return pl.pallas_call(
        pre_kernel,
        out_shape=jax.ShapeDtypeStruct((128, 32, LANES), jnp.float32),
        in_specs=[
            pl.BlockSpec(memory_space=pltpu.SMEM),
            pl.BlockSpec(memory_space=pltpu.HBM),
        ],
        out_specs=pl.BlockSpec(memory_space=pltpu.HBM),
        scratch_shapes=[
            pltpu.VMEM((2, 16, 128, LANES), jnp.float32),
            pltpu.VMEM((128, 32, LANES), jnp.float32),
            pltpu.VMEM((16, LANES), jnp.float32),
            pltpu.VMEM((16, LANES), jnp.float32),
            pltpu.VMEM((128, LANES), jnp.float32),
            pltpu.VMEM((128, LANES), jnp.float32),
            pltpu.SemaphoreType.DMA((PARTS,)),
            pltpu.SemaphoreType.DMA((PARTS,)),
        ],
        compiler_params=pltpu.CompilerParams(vmem_limit_bytes=60 * MIB),
        cost_estimate=pl.CostEstimate(
            flops=10 * MIB, bytes_accessed=4 * MIB, transcendentals=0
        ),
    )(deform, coeffs)


def phase_rows(tables, deform, store):
    y1, y2 = warp(deform, tables[0], tables[1])
    c, s = turn(tables[2] * y1 + tables[3] * y2)
    real = tables[4] < 0.5
    for child in range(2):
        sine_part = s if child else -s
        store[child, 0] = jnp.where(real, c, sine_part)
        store[child, 1] = jnp.where(real, -sine_part, c)


def dot(a, b):
    return jnp.dot(a, b, precision=lax.Precision.HIGHEST, preferred_element_type=jnp.float32)


def level(pattern, rows, child, part):
    shape = pattern.shape
    real = (iota(shape, 0) & POINTS) == 0
    return pattern * jnp.where(real, rows[child][0][:, part], rows[child][1][:, part])


def build_kernel(
    deform, inner, outer, wide, px, py, px_last, m1_out, m2_out, first, second, rows_in, rows_out, m1, m2, sems
):
    phase_rows(inner, deform, rows_in)
    phase_rows(outer, deform, rows_out)

    def chain(rows, at_x, at_y, at_last):
        last = jnp.concatenate(
            [level(px_last[...], rows, c, slice(at_last, at_last + 64)) for c in range(2)], axis=0
        )
        parts = [dot(last, level(py[...], rows, c, slice(at_y, at_y + 128))) for c in range(2)]
        joined = jnp.concatenate(
            [parts[cy][32 * cx : 32 * cx + 32] for cx in range(2) for cy in range(2)], axis=0
        )
        return [
            dot(joined, level(px[...], rows, c, slice(at_x, at_x + 256))) for c in range(2)
        ]

    def group(g, carry):
        rows = [[rows_in[c, z, pl.ds(g, 1), :] for z in range(2)] for c in range(2)]
        for c, value in enumerate(chain(rows, 0, 256, 384)):
            high, low = split(value)
            m1[g, pl.ds(128 * c, 128), :] = high
            m1[g, pl.ds(256 + 128 * c, 128), :] = low
        return carry

    lax.fori_loop(0, 16, group, 0)
    copies = [
        pltpu.make_async_copy(m1, m1_out, sems.at[0]),
        pltpu.make_async_copy(m2, m2_out, sems.at[1]),
    ]
    copies[0].start()

    rows = [[rows_out[c, z, 0:1, :] for z in range(2)] for c in range(2)]
    for c5, value in enumerate(chain(rows, 512, 768, 896)):
        for c4 in range(2):
            block = dot(value, level(wide[...], rows, c4, slice(0, 512)))
            for c7 in range(2):
                for c6 in range(2):
                    high, low = split(block[64 * c7 + 32 * c6 : 64 * c7 + 32 * c6 + 32])
                    at = 32 * (8 * c5 + 4 * c7 + 2 * c4 + c6)
                    m2[0, pl.ds(at, 32), :] = high
                    m2[1, pl.ds(at, 32), :] = low

    copies[1].start()
    sx = lax.axis_index("sx").astype(jnp.float32)
    sy = lax.axis_index("sy").astype(jnp.float32)
    y1, y2 = warp(deform, *lane_nodes())
    c, s = turn(y1[0:1] * (iota((16, LANES), 0).astype(jnp.float32) + (16.0 * sx + 0.5)))
    scale = math.sqrt(0.5) ** 7
    first[0] = c * scale
    first[1] = s * scale
    c, s = turn(y2[0:1] * (iota((128, LANES), 0).astype(jnp.float32) + (128.0 * sy + 0.5)))
    second[0] = c
    second[1] = s
    for copy in copies:
        copy.wait()


def build(deform):
    inner, outer = column_tables()
    consts = [inner, outer, pattern_y_first(), pattern_x(), pattern_y(), pattern_x_last()]
    vmem = pl.BlockSpec(memory_space=pltpu.VMEM)
    return pl.pallas_call(
        build_kernel,
        out_shape=[
            pltpu.HBM((16, 512, 256), jnp.bfloat16),
            pltpu.HBM((2, 512, 512), jnp.bfloat16),
            jax.ShapeDtypeStruct((2, 16, LANES), jnp.float32),
            jax.ShapeDtypeStruct((2, 128, LANES), jnp.float32),
        ],
        in_specs=[pl.BlockSpec(memory_space=pltpu.SMEM)] + [vmem] * 6,
        out_specs=[pl.BlockSpec(memory_space=pltpu.HBM)] * 2 + [vmem] * 2,
        scratch_shapes=[
            pltpu.VMEM((2, 2, 16, 512), jnp.float32),
            pltpu.VMEM((2, 2, 8, 1024), jnp.float32),
            pltpu.VMEM((16, 512, 256), jnp.bfloat16),
            pltpu.VMEM((2, 512, 512), jnp.bfloat16),
            pltpu.SemaphoreType.DMA((2,)),
        ],
        compiler_params=pltpu.CompilerParams(vmem_limit_bytes=16 * MIB),
        cost_estimate=pl.CostEstimate(
            flops=6000 * MIB, bytes_accessed=40 * MIB, transcendentals=0
        ),
    )(deform, *[jnp.asarray(c, dtype=jnp.float32) for c in consts])


def mul(a, b):
    return jnp.dot(a, b, preferred_element_type=jnp.float32)


def post_kernel(
    m1_in, m2_in, first, second, got, out, m1, m2, high, low, acc, done, cos, sin, sems, in_sems
):
    loads = [
        pltpu.make_async_copy(m1_in.at[pl.ds(4 * p, 4)], m1.at[pl.ds(4 * p, 4)], in_sems.at[p])
        for p in range(4)
    ] + [pltpu.make_async_copy(m2_in, m2, in_sems.at[4])]
    for load in loads:
        load.start()

    def stage_one(g, carry):
        gx, gy = g // 4, g % 4
        x = jnp.concatenate(
            [got[pl.ds((4 * gx + i) * 8 + 2 * gy, 2)].reshape(64, LANES) for i in range(4)], axis=0
        )
        xh, xl = split(x)
        res = mul(m1[g], jnp.concatenate([xh, xl], axis=1))
        res = res[:256, :128] + (res[:256, 128:] + res[256:, :128])
        yh, yl = split(res)
        for c13 in range(4):
            for c2 in range(2):
                piece = slice(64 * c13 + 32 * c2, 64 * c13 + 32 * c2 + 32)
                at = pl.ds(pl.multiple_of(32 * g, 32), 32)
                high[c13, at, pl.ds(128 * c2, 128)] = yh[piece]
                low[c13, at, pl.ds(128 * c2, 128)] = yl[piece]
        return carry

    for p in range(4):
        loads[p].wait()
        lax.fori_loop(4 * p, 4 * p + 4, stage_one, 0, unroll=4)
    loads[4].wait()

    maps = flip_maps()

    def copies(c13):
        return [
            pltpu.make_async_copy(
                done.at[z, pl.ds(4 * c13, 4)], out.at[z, pl.ds(4 * c13, 4)], sems.at[z, c13]
            )
            for z in range(2)
        ]

    for c13 in range(4):
        acc[...] = mul(m2[0], high[c13]) + (mul(m2[0], low[c13]) + mul(m2[1], high[c13]))

        def finish(c57, carry):
            cx = 4 * c13 + c57
            c1, s1 = first[0, pl.ds(cx, 1), :], first[1, pl.ds(cx, 1), :]
            c2, s2 = second[0], second[1]
            c = c1 * c2 - s1 * s2
            s = s1 * c2 + c1 * s2
            cos[...] = c
            sin[...] = s
            for cy in range(8):
                at = pl.multiple_of(128 * c57, 128) + 32 * (cy & 3)
                part = pl.ds(128 * (cy >> 2), 128)
                re, im = [
                    flip(
                        acc[pl.ds(at + 16 * z, 8), part],
                        acc[pl.ds(at + 16 * z + 8, 8), part],
                        maps,
                    )
                    for z in range(2)
                ]
                for half in range(2):
                    rows = pl.ds(64 * half + cy, 8, stride=8)
                    c, s = cos[rows, :], sin[rows, :]
                    done[0, cx, rows, :] = re[half] * c - im[half] * s
                    done[1, cx, rows, :] = im[half] * c + re[half] * s
            return carry

        lax.fori_loop(0, 4, finish, 0, unroll=4)
        for copy in copies(c13):
            copy.start()
    for c13 in range(4):
        for copy in copies(c13):
            copy.wait()


def post(m1, m2, first, second, got):
    vmem = pl.BlockSpec(memory_space=pltpu.VMEM)
    return pl.pallas_call(
        post_kernel,
        out_shape=jax.ShapeDtypeStruct((2, 16, 128, LANES), jnp.float32),
        in_specs=[pl.BlockSpec(memory_space=pltpu.HBM)] * 2 + [vmem] * 3,
        out_specs=pl.BlockSpec(memory_space=pltpu.HBM),
        scratch_shapes=[
            pltpu.VMEM((16, 512, 256), jnp.bfloat16),
            pltpu.VMEM((2, 512, 512), jnp.bfloat16),
            pltpu.VMEM((4, 512, 256), jnp.bfloat16),
            pltpu.VMEM((4, 512, 256), jnp.bfloat16),
            pltpu.VMEM((512, 256), jnp.float32),
            pltpu.VMEM((2, 16, 128, LANES), jnp.float32),
            pltpu.VMEM((128, LANES), jnp.float32),
            pltpu.VMEM((128, LANES), jnp.float32),
            pltpu.SemaphoreType.DMA((2, 4)),
            pltpu.SemaphoreType.DMA((5,)),
        ],
        compiler_params=pltpu.CompilerParams(vmem_limit_bytes=16 * MIB),
        cost_estimate=pl.CostEstimate(
            flops=4000 * MIB, bytes_accessed=10 * MIB, transcendentals=0
        ),
    )(*[pltpu.with_memory_space_constraint(m, pltpu.HBM) for m in (m1, m2)], first, second, got)


def body(coeffs, deform):
    sent = pre(coeffs, deform)
    got = lax.all_to_all(sent, ("sx", "sy"), 0, 0, tiled=True)
    return post(*build(deform), got)


def solution(mesh):
    placed = (P(None, "sx", None, "sy", None, None), P())
    return jax.shard_map(
        body, mesh=mesh, in_specs=placed, out_specs=P(None, "sx", "sy", None), check_vma=False
    )
```

```python
import math

import jax
import jax.numpy as jnp
import numpy as np
from jax import lax
from jax.experimental import pallas as pl
from jax.experimental.pallas import tpu as pltpu
from jax.sharding import Mesh
from jax.sharding import PartitionSpec as P

NODES = 4
RHS = 8
POINTS = NODES * NODES
LANES = RHS * POINTS
MIB = 1 << 20


def cheb_nodes(count):
    return (1.0 - np.cos(np.pi * (2.0 * np.arange(count) + 1.0) / (2.0 * count))) / 2.0


def lagrange_table(count):
    nodes = cheb_nodes(count)
    table = np.ones((count, 2, count))
    for row in range(count):
        for sibling in range(2):
            spots = (sibling + nodes) / 2.0
            for other in range(count):
                if other != row:
                    table[row, sibling] *= (spots - nodes[other]) / (nodes[row] - nodes[other])
    return table


def pattern_x():
    L, e2, e4, one = lagrange_table(NODES), np.eye(2), np.eye(NODES), np.ones((2, 2))
    return np.einsum("hH,yY,zZ,asu,vV->hyzavHsYZuV", e2, e2, one, L, e4).reshape(128, 256)


def pattern_y():
    L, e2, e4, one = lagrange_table(NODES), np.eye(2), np.eye(NODES), np.ones((2, 2))
    return np.einsum("hH,zZ,aA,bsv->hzabHsZAv", e2, one, e4, L).reshape(64, 128)


def pattern_x_last():
    L, e4, one = lagrange_table(NODES), np.eye(NODES), np.ones((2, 2))
    return np.einsum("zZ,asu,bB->zabsZuB", one, L, e4).reshape(32, 64)


def pattern_y_first():
    L, e2, e4, one = lagrange_table(NODES), np.eye(2), np.eye(NODES), np.ones((2, 2))
    return np.einsum("gG,hH,zZ,uU,bsv->ghzubGHsZUv", e4, e2, one, e4, L).reshape(256, 512)


def columns(dims, first, second, first_turns, second_turns):
    names, sizes = zip(*dims)
    grid = dict(zip(names, np.meshgrid(*[np.arange(s) for s in sizes], indexing="ij")))
    shape = grid["z"].shape
    flat = lambda v: np.broadcast_to(v, shape).reshape(-1)
    return np.stack(
        [flat(first(grid)), flat(second(grid)), flat(first_turns), flat(second_turns), flat(grid["z"])]
    )


def column_tables():
    q = cheb_nodes(NODES)
    groups = []
    for gx in range(4):
        for gy in range(4):
            one = columns(
                [("h", 2), ("l", 2), ("y", 2), ("z", 2), ("u", 4), ("v", 4)],
                lambda g: (4 * gx + 2 * g["h"] + g["l"] + q[g["u"]]) / 16,
                lambda g: (2 * gy + g["y"] + q[g["v"]]) / 8,
                4.0,
                0.0,
            )
            two = columns(
                [("h", 2), ("y", 2), ("z", 2), ("u", 4), ("v", 4)],
                lambda g: (2 * gx + g["h"] + q[g["u"]]) / 8,
                lambda g: (2 * gy + g["y"] + q[g["v"]]) / 8,
                0.0,
                2.0,
            )
            three = columns(
                [("h", 2), ("z", 2), ("u", 4), ("v", 4)],
                lambda g: (2 * gx + g["h"] + q[g["u"]]) / 8,
                lambda g: (gy + q[g["v"]]) / 4,
                2.0,
                0.0,
            )
            groups.append(np.concatenate([one, two, three, np.zeros((5, 64))], axis=1))
    inner = np.stack(groups, axis=1)
    four = columns(
        [("g", 4), ("h", 2), ("l", 2), ("z", 2), ("u", 4), ("v", 4)],
        lambda g: (g["g"] + q[g["u"]]) / 4,
        lambda g: (2 * g["h"] + g["l"] + q[g["v"]]) / 4,
        0.0,
        1.0,
    )
    five = columns(
        [("h", 2), ("l", 2), ("y", 2), ("z", 2), ("u", 4), ("v", 4)],
        lambda g: (2 * g["h"] + g["l"] + q[g["u"]]) / 4,
        lambda g: (g["y"] + q[g["v"]]) / 2,
        1.0,
        0.0,
    )
    six = columns(
        [("h", 2), ("y", 2), ("z", 2), ("u", 4), ("v", 4)],
        lambda g: (g["h"] + q[g["u"]]) / 2,
        lambda g: (g["y"] + q[g["v"]]) / 2,
        0.0,
        0.5,
    )
    seven = columns(
        [("h", 2), ("z", 2), ("u", 4), ("v", 4)],
        lambda g: (g["h"] + q[g["u"]]) / 2,
        lambda g: q[g["v"]] + 0.0 * g["h"],
        0.5,
        0.0,
    )
    outer = np.concatenate([four, five, six, seven, np.zeros((5, 64))], axis=1)
    outer = np.broadcast_to(outer[:, None], (5, 8, 1024))
    return inner.astype(np.float32), outer.astype(np.float32)


SINE = [
    (-1) ** k * (2.0 * math.pi) ** (2 * k + 1) / math.factorial(2 * k + 1) for k in range(7)
]


def sine_quarter(x):
    square = x * x
    total = jnp.full_like(x, SINE[-1])
    for coefficient in SINE[-2::-1]:
        total = total * square + coefficient
    return total * x


def turn(x):
    part = x - jnp.round(x)
    size = jnp.abs(part)
    folded = jnp.where(size > 0.25, jnp.where(part > 0, 0.5, -0.5) - part, part)
    return sine_quarter(0.25 - size), sine_quarter(folded)


def sine(x):
    part = x - jnp.round(x)
    folded = jnp.where(jnp.abs(part) > 0.25, jnp.where(part > 0, 0.5, -0.5) - part, part)
    return sine_quarter(folded)


def warp(deform, first, second):
    total, differ = 0.5 * (first + second), 0.5 * (first - second)
    y1, y2 = None, None
    for m in range(4):
        one = deform[0, m] * sine(total * (m + 1.0))
        two = deform[1, m] * sine(differ * (m + 1.0))
        y1 = one if y1 is None else y1 + one
        y2 = two if y2 is None else y2 + two
    return first + y1, second + y2


def flip_maps():
    row, lane = iota((8, LANES), 0), iota((8, LANES), 1)
    spot = lane & 15
    back, on = row - spot, row + spot
    lanes = [(lane & ~15) | ((back + 8 * half) & 15) for half in range(2)]
    return back & 7, (back & 8) == 0, lanes, on & 7, (on & 8) == 0


def flip(low, high, maps):
    rows, first, lanes, rows_back, first_back = maps

    def spread(x, y, rows, first):
        x = jnp.take_along_axis(x, rows, axis=0)
        y = jnp.take_along_axis(y, rows, axis=0)
        return jnp.where(first, x, y), jnp.where(first, y, x)

    low, high = spread(low, high, rows, first)
    low = jnp.take_along_axis(low, lanes[0], axis=1)
    high = jnp.take_along_axis(high, lanes[1], axis=1)
    return spread(low, high, rows_back, first_back)


def split(x):
    high = x.astype(jnp.bfloat16)
    low = (x - high.astype(jnp.float32)).astype(jnp.bfloat16)
    return high, low


def lane_nodes():
    lane = iota((8, LANES), 1)
    q = [float(v) for v in cheb_nodes(NODES)]

    def pick(t):
        return jnp.where(t < 2, jnp.where(t == 0, q[0], q[1]), jnp.where(t == 2, q[2], q[3]))

    return pick((lane >> 2) & 3), pick(lane & 3)


def position():
    at = lax.axis_index
    return at("x_hi") * 8 + at("y") * 2 + at("core"), at("z") * 2 + at("x_lo")


def iota(shape, dim):
    return lax.broadcasted_iota(jnp.int32, shape, dim)


PARTS = 8
CHUNKS = (2, 4, 4, 2, 64, LANES)


def pre_kernel(deform, coeffs, out, held, ready, first_cos, first_sin, second_cos, second_sin, sems, out_sems):
    copies = [
        pltpu.make_async_copy(
            coeffs.at[:, 0, pl.ds(2 * p, 2), 0], held.at[:, pl.ds(2 * p, 2)], sems.at[p]
        )
        for p in range(PARTS)
    ]
    sends = [
        pltpu.make_async_copy(
            ready.at[:, :, p & 3, p >> 2], out.at[:, :, p & 3, p >> 2], out_sems.at[p]
        )
        for p in range(PARTS)
    ]
    for copy in copies:
        copy.start()

    nodes = lane_nodes()
    sx, sy = [v.astype(jnp.float32) for v in position()]
    y1, y2 = warp(deform, (nodes[0] + sx) * (1 / 16), (nodes[1] + sy) * (1 / 8))
    y1, y2 = y1[0:1] * 16.0, y2[0:1] * 8.0
    first_cos[...], first_sin[...] = turn(y1 * (iota((16, LANES), 0).astype(jnp.float32) + 0.5))
    second_cos[...], second_sin[...] = turn(y2 * (iota((128, LANES), 0).astype(jnp.float32) + 0.5))
    maps = flip_maps()

    def one(b1):
        c1, s1 = first_cos[b1 : b1 + 1, :], first_sin[b1 : b1 + 1, :]
        for k in range(8):
            turned = []
            for half in range(2):
                at = pl.ds(16 * k + 8 * half, 8)
                c2, s2 = second_cos[at, :], second_sin[at, :]
                c = c1 * c2 - s1 * s2
                s = s1 * c2 + c1 * s2
                re, im = held[0, b1, at, :], held[1, b1, at, :]
                turned.append((re * c + im * s, im * c - re * s))
            for z in range(2):
                low, high = flip(turned[0][z], turned[1][z], maps)
                at = 32 * (k & 1) + 16 * z
                spot = (b1 & 1, k >> 1, (b1 >> 1) & 3, b1 >> 3)
                ready[(*spot, pl.ds(at, 8))] = low
                ready[(*spot, pl.ds(at + 8, 8))] = high

    for q in range(0, PARTS, 2):
        for p in (q, q + 1):
            copies[p].wait()
        for b1 in range(2 * q, 2 * q + 4):
            one(b1)
        for p in (q, q + 1):
            sends[p].start()
    for send in sends:
        send.wait()


def pre(coeffs, deform):
    return pl.pallas_call(
        pre_kernel,
        out_shape=jax.ShapeDtypeStruct(CHUNKS, jnp.float32),
        in_specs=[
            pl.BlockSpec(memory_space=pltpu.SMEM),
            pl.BlockSpec(memory_space=pltpu.HBM),
        ],
        out_specs=pl.BlockSpec(memory_space=pltpu.HBM),
        scratch_shapes=[
            pltpu.VMEM((2, 16, 128, LANES), jnp.float32),
            pltpu.VMEM(CHUNKS, jnp.float32),
            pltpu.VMEM((16, LANES), jnp.float32),
            pltpu.VMEM((16, LANES), jnp.float32),
            pltpu.VMEM((128, LANES), jnp.float32),
            pltpu.VMEM((128, LANES), jnp.float32),
            pltpu.SemaphoreType.DMA((PARTS,)),
            pltpu.SemaphoreType.DMA((PARTS,)),
        ],
        compiler_params=pltpu.CompilerParams(vmem_limit_bytes=60 * MIB),
        cost_estimate=pl.CostEstimate(
            flops=10 * MIB, bytes_accessed=4 * MIB, transcendentals=0
        ),
    )(deform, coeffs)


def phase_rows(tables, deform, store):
    y1, y2 = warp(deform, tables[0], tables[1])
    c, s = turn(tables[2] * y1 + tables[3] * y2)
    real = tables[4] < 0.5
    for child in range(2):
        sine_part = s if child else -s
        store[child, 0] = jnp.where(real, c, sine_part)
        store[child, 1] = jnp.where(real, -sine_part, c)


def dot(a, b):
    return jnp.dot(a, b, precision=lax.Precision.HIGHEST, preferred_element_type=jnp.float32)


def level(pattern, rows, child, part):
    shape = pattern.shape
    real = (iota(shape, 0) & POINTS) == 0
    return pattern * jnp.where(real, rows[child][0][:, part], rows[child][1][:, part])


def build_kernel(
    deform, inner, outer, wide, px, py, px_last, m1_out, m2_out, first, second, rows_in, rows_out, m1, m2, sems
):
    phase_rows(inner, deform, rows_in)
    phase_rows(outer, deform, rows_out)

    def chain(rows, at_x, at_y, at_last, keep):
        last = jnp.concatenate(
            [level(px_last[...], rows, c, slice(at_last, at_last + 64)) for c in range(2)], axis=0
        )
        parts = [dot(last, level(py[...], rows, c, slice(at_y, at_y + 128))) for c in range(2)]
        joined = jnp.concatenate(
            [parts[cy][32 * cx : 32 * cx + keep] for cx in range(2) for cy in range(2)], axis=0
        )
        return [
            dot(joined, level(px[...], rows, c, slice(at_x, at_x + 256))) for c in range(2)
        ]

    def group(g, carry):
        rows = [[rows_in[c, z, pl.ds(g, 1), :] for z in range(2)] for c in range(2)]
        for c, value in enumerate(chain(rows, 0, 256, 384, 16)):
            high, low = split(value)
            m1[g, pl.ds(64 * c, 64), :] = high
            m1[g, pl.ds(128 + 64 * c, 64), :] = low
        return carry

    lax.fori_loop(0, 16, group, 0)
    copies = [
        pltpu.make_async_copy(m1, m1_out, sems.at[0]),
        pltpu.make_async_copy(m2, m2_out, sems.at[1]),
    ]
    copies[0].start()

    rows = [[rows_out[c, z, 0:1, :] for z in range(2)] for c in range(2)]
    for c5, value in enumerate(chain(rows, 512, 768, 896, 32)):
        for c4 in range(2):
            block = dot(value, level(wide[...], rows, c4, slice(0, 512)))
            for c7 in range(2):
                for c6 in range(2):
                    high, low = split(block[64 * c7 + 32 * c6 : 64 * c7 + 32 * c6 + 32])
                    at = 32 * (8 * c5 + 4 * c7 + 2 * c4 + c6)
                    m2[0, pl.ds(at, 32), :] = high
                    m2[1, pl.ds(at, 32), :] = low

    copies[1].start()
    sx, sy = [v.astype(jnp.float32) for v in position()]
    y1, y2 = warp(deform, *lane_nodes())
    c, s = turn(y1[0:1] * (iota((16, LANES), 0).astype(jnp.float32) + (16.0 * sx + 0.5)))
    scale = math.sqrt(0.5) ** 7
    first[0] = c * scale
    first[1] = s * scale
    c, s = turn(y2[0:1] * (iota((128, LANES), 0).astype(jnp.float32) + (128.0 * sy + 0.5)))
    second[0] = c
    second[1] = s
    for copy in copies:
        copy.wait()


def build(deform):
    inner, outer = column_tables()
    consts = [inner, outer, pattern_y_first(), pattern_x(), pattern_y(), pattern_x_last()]
    vmem = pl.BlockSpec(memory_space=pltpu.VMEM)
    return pl.pallas_call(
        build_kernel,
        out_shape=[
            pltpu.HBM((16, 256, 256), jnp.bfloat16),
            pltpu.HBM((2, 512, 512), jnp.bfloat16),
            jax.ShapeDtypeStruct((2, 16, LANES), jnp.float32),
            jax.ShapeDtypeStruct((2, 128, LANES), jnp.float32),
        ],
        in_specs=[pl.BlockSpec(memory_space=pltpu.SMEM)] + [vmem] * 6,
        out_specs=[pl.BlockSpec(memory_space=pltpu.HBM)] * 2 + [vmem] * 2,
        scratch_shapes=[
            pltpu.VMEM((2, 2, 16, 512), jnp.float32),
            pltpu.VMEM((2, 2, 8, 1024), jnp.float32),
            pltpu.VMEM((16, 256, 256), jnp.bfloat16),
            pltpu.VMEM((2, 512, 512), jnp.bfloat16),
            pltpu.SemaphoreType.DMA((2,)),
        ],
        compiler_params=pltpu.CompilerParams(vmem_limit_bytes=16 * MIB),
        cost_estimate=pl.CostEstimate(
            flops=6000 * MIB, bytes_accessed=40 * MIB, transcendentals=0
        ),
    )(deform, *[jnp.asarray(c, dtype=jnp.float32) for c in consts])


def mul(a, b):
    return jnp.dot(a, b, preferred_element_type=jnp.float32)


def post_kernel(
    m1_in, m2_in, first, second, got, out, m1, m2, high, low, acc, done, cos, sin, sems, in_sems
):
    loads = [
        pltpu.make_async_copy(m1_in.at[pl.ds(8 * p, 8)], m1.at[pl.ds(8 * p, 8)], in_sems.at[p])
        for p in range(2)
    ] + [pltpu.make_async_copy(m2_in, m2, in_sems.at[2])]
    for load in loads:
        load.start()

    def stage_one(g, matrix):
        gx, gy = g >> 2, g & 3
        x = [[], []]
        for i in range(4):
            chunk = (i & 1) * 64 + gy * 16 + ((gx & 1) * 2 + (i >> 1)) * 4 + (gx >> 1) * 2
            for j in range(2):
                re, im = got[chunk + j, 0:16, :], got[chunk + j, 16:32, :]
                x[0] += [re, im]
                x[1] += [im, -re]
        x = [split(jnp.concatenate(v, axis=0)) for v in x]
        res = mul(matrix, jnp.concatenate([*x[0], *x[1]], axis=1))
        for z in range(2):
            part = res[:, 256 * z : 256 * z + 256]
            yh, yl = split(part[:128, :128] + (part[:128, 128:] + part[128:, :128]))
            at = pl.ds(32 * g + 16 * z, 16)
            for c13 in range(4):
                for c2 in range(2):
                    piece = slice(32 * c13 + 16 * c2, 32 * c13 + 16 * c2 + 16)
                    high[c13, at, pl.ds(128 * c2, 128)] = yh[piece]
                    low[c13, at, pl.ds(128 * c2, 128)] = yl[piece]

    for p in range(2):
        loads[p].wait()
        for g in range(8 * p, 8 * p + 8):
            stage_one(g, m1[g])
    loads[2].wait()

    maps = flip_maps()

    def copies(c13):
        return [
            pltpu.make_async_copy(
                done.at[z, pl.ds(4 * c13, 4)], out.at[z, pl.ds(4 * c13, 4)], sems.at[z, c13]
            )
            for z in range(2)
        ]

    for c13 in range(4):
        acc[...] = mul(m2[0], high[c13]) + (mul(m2[0], low[c13]) + mul(m2[1], high[c13]))

        def finish(c57, carry):
            cx = 4 * c13 + c57
            c1, s1 = first[0, pl.ds(cx, 1), :], first[1, pl.ds(cx, 1), :]
            c2, s2 = second[0], second[1]
            c = c1 * c2 - s1 * s2
            s = s1 * c2 + c1 * s2
            cos[...] = c
            sin[...] = s
            for cy in range(8):
                at = pl.multiple_of(128 * c57, 128) + 32 * (cy & 3)
                part = pl.ds(128 * (cy >> 2), 128)
                re, im = [
                    flip(
                        acc[pl.ds(at + 16 * z, 8), part],
                        acc[pl.ds(at + 16 * z + 8, 8), part],
                        maps,
                    )
                    for z in range(2)
                ]
                for half in range(2):
                    rows = pl.ds(64 * half + cy, 8, stride=8)
                    c, s = cos[rows, :], sin[rows, :]
                    done[0, cx, rows, :] = re[half] * c - im[half] * s
                    done[1, cx, rows, :] = im[half] * c + re[half] * s
            return carry

        lax.fori_loop(0, 4, finish, 0, unroll=4)
        for copy in copies(c13):
            copy.start()
    for c13 in range(4):
        for copy in copies(c13):
            copy.wait()


def post(m1, m2, first, second, got):
    vmem = pl.BlockSpec(memory_space=pltpu.VMEM)
    return pl.pallas_call(
        post_kernel,
        out_shape=jax.ShapeDtypeStruct((2, 16, 128, LANES), jnp.float32),
        in_specs=[pl.BlockSpec(memory_space=pltpu.HBM)] * 2 + [vmem] * 3,
        out_specs=pl.BlockSpec(memory_space=pltpu.HBM),
        scratch_shapes=[
            pltpu.VMEM((16, 256, 256), jnp.bfloat16),
            pltpu.VMEM((2, 512, 512), jnp.bfloat16),
            pltpu.VMEM((4, 512, 256), jnp.bfloat16),
            pltpu.VMEM((4, 512, 256), jnp.bfloat16),
            pltpu.VMEM((512, 256), jnp.float32),
            pltpu.VMEM((2, 16, 128, LANES), jnp.float32),
            pltpu.VMEM((128, LANES), jnp.float32),
            pltpu.VMEM((128, LANES), jnp.float32),
            pltpu.SemaphoreType.DMA((2, 4)),
            pltpu.SemaphoreType.DMA((3,)),
        ],
        compiler_params=pltpu.CompilerParams(vmem_limit_bytes=16 * MIB),
        cost_estimate=pl.CostEstimate(
            flops=4000 * MIB, bytes_accessed=10 * MIB, transcendentals=0
        ),
    )(
        *[pltpu.with_memory_space_constraint(m, pltpu.HBM) for m in (m1, m2)],
        first,
        second,
        got,
    )


def body(coeffs, deform):
    sent = pre(coeffs, deform)
    sent = sent.reshape(128, 32, LANES)
    got = lax.all_to_all(sent, ("core", "z", "y", "x_hi", "x_lo"), 0, 0, tiled=True)
    return post(*build(deform), got)


def solution(mesh):
    fine = Mesh(mesh.devices.reshape(2, 4, 2, 4, 2), ("x_hi", "y", "core", "z", "x_lo"))
    sx, sy = ("x_hi", "y", "core"), ("z", "x_lo")
    return jax.shard_map(
        body,
        mesh=fine,
        in_specs=(P(None, sx, None, sy, None, None), P()),
        out_specs=P(None, sx, sy, None),
        check_vma=False,
    )
```

```python
import math

import jax
import jax.numpy as jnp
import numpy as np
from jax import lax
from jax.experimental import pallas as pl
from jax.experimental.pallas import tpu as pltpu
from jax.sharding import Mesh
from jax.sharding import PartitionSpec as P

NODES = 4
RHS = 8
POINTS = NODES * NODES
LANES = RHS * POINTS
MIB = 1 << 20


def cheb_nodes(count):
    return (1.0 - np.cos(np.pi * (2.0 * np.arange(count) + 1.0) / (2.0 * count))) / 2.0


def lagrange_table(count):
    nodes = cheb_nodes(count)
    table = np.ones((count, 2, count))
    for row in range(count):
        for sibling in range(2):
            spots = (sibling + nodes) / 2.0
            for other in range(count):
                if other != row:
                    table[row, sibling] *= (spots - nodes[other]) / (nodes[row] - nodes[other])
    return table


def pattern_x():
    L, e2, e4, one = lagrange_table(NODES), np.eye(2), np.eye(NODES), np.ones((2, 2))
    return np.einsum("hH,yY,zZ,asu,vV->hyzavHsYZuV", e2, e2, one, L, e4).reshape(128, 256)


def pattern_y():
    L, e2, e4, one = lagrange_table(NODES), np.eye(2), np.eye(NODES), np.ones((2, 2))
    return np.einsum("hH,zZ,aA,bsv->hzabHsZAv", e2, one, e4, L).reshape(64, 128)


def pattern_x_last():
    L, e4, one = lagrange_table(NODES), np.eye(NODES), np.ones((2, 2))
    return np.einsum("zZ,asu,bB->zabsZuB", one, L, e4).reshape(32, 64)


def pattern_y_first():
    L, e2, e4, one = lagrange_table(NODES), np.eye(2), np.eye(NODES), np.ones((2, 2))
    return np.einsum("gG,hH,zZ,uU,bsv->ghzubGHsZUv", e4, e2, one, e4, L).reshape(256, 512)


def columns(dims, first, second, first_turns, second_turns):
    names, sizes = zip(*dims)
    grid = dict(zip(names, np.meshgrid(*[np.arange(s) for s in sizes], indexing="ij")))
    shape = grid["z"].shape
    flat = lambda v: np.broadcast_to(v, shape).reshape(-1)
    return np.stack(
        [flat(first(grid)), flat(second(grid)), flat(first_turns), flat(second_turns), flat(grid["z"])]
    )


def column_tables():
    q = cheb_nodes(NODES)
    groups = []
    for gx in range(4):
        for gy in range(4):
            one = columns(
                [("h", 2), ("l", 2), ("y", 2), ("z", 2), ("u", 4), ("v", 4)],
                lambda g: (4 * gx + 2 * g["h"] + g["l"] + q[g["u"]]) / 16,
                lambda g: (2 * gy + g["y"] + q[g["v"]]) / 8,
                4.0,
                0.0,
            )
            two = columns(
                [("h", 2), ("y", 2), ("z", 2), ("u", 4), ("v", 4)],
                lambda g: (2 * gx + g["h"] + q[g["u"]]) / 8,
                lambda g: (2 * gy + g["y"] + q[g["v"]]) / 8,
                0.0,
                2.0,
            )
            three = columns(
                [("h", 2), ("z", 2), ("u", 4), ("v", 4)],
                lambda g: (2 * gx + g["h"] + q[g["u"]]) / 8,
                lambda g: (gy + q[g["v"]]) / 4,
                2.0,
                0.0,
            )
            groups.append(np.concatenate([one, two, three, np.zeros((5, 64))], axis=1))
    inner = np.stack(groups, axis=1)
    four = columns(
        [("g", 4), ("h", 2), ("l", 2), ("z", 2), ("u", 4), ("v", 4)],
        lambda g: (g["g"] + q[g["u"]]) / 4,
        lambda g: (2 * g["h"] + g["l"] + q[g["v"]]) / 4,
        0.0,
        1.0,
    )
    five = columns(
        [("h", 2), ("l", 2), ("y", 2), ("z", 2), ("u", 4), ("v", 4)],
        lambda g: (2 * g["h"] + g["l"] + q[g["u"]]) / 4,
        lambda g: (g["y"] + q[g["v"]]) / 2,
        1.0,
        0.0,
    )
    six = columns(
        [("h", 2), ("y", 2), ("z", 2), ("u", 4), ("v", 4)],
        lambda g: (g["h"] + q[g["u"]]) / 2,
        lambda g: (g["y"] + q[g["v"]]) / 2,
        0.0,
        0.5,
    )
    seven = columns(
        [("h", 2), ("z", 2), ("u", 4), ("v", 4)],
        lambda g: (g["h"] + q[g["u"]]) / 2,
        lambda g: q[g["v"]] + 0.0 * g["h"],
        0.5,
        0.0,
    )
    outer = np.concatenate([four, five, six, seven, np.zeros((5, 64))], axis=1)
    outer = np.broadcast_to(outer[:, None], (5, 8, 1024))
    return inner.astype(np.float32), outer.astype(np.float32)


SINE = [
    (-1) ** k * (2.0 * math.pi) ** (2 * k + 1) / math.factorial(2 * k + 1) for k in range(7)
]


def sine_quarter(x):
    square = x * x
    total = jnp.full_like(x, SINE[-1])
    for coefficient in SINE[-2::-1]:
        total = total * square + coefficient
    return total * x


def turn(x):
    part = x - jnp.round(x)
    size = jnp.abs(part)
    folded = jnp.where(size > 0.25, jnp.where(part > 0, 0.5, -0.5) - part, part)
    return sine_quarter(0.25 - size), sine_quarter(folded)


def sine(x):
    part = x - jnp.round(x)
    folded = jnp.where(jnp.abs(part) > 0.25, jnp.where(part > 0, 0.5, -0.5) - part, part)
    return sine_quarter(folded)


def warp(deform, first, second):
    total, differ = 0.5 * (first + second), 0.5 * (first - second)
    y1, y2 = None, None
    for m in range(4):
        one = deform[0, m] * sine(total * (m + 1.0))
        two = deform[1, m] * sine(differ * (m + 1.0))
        y1 = one if y1 is None else y1 + one
        y2 = two if y2 is None else y2 + two
    return first + y1, second + y2


def flip_maps():
    row, lane = iota((8, LANES), 0), iota((8, LANES), 1)
    spot = lane & 15
    back, on = row - spot, row + spot
    lanes = [(lane & ~15) | ((back + 8 * half) & 15) for half in range(2)]
    return back & 7, (back & 8) == 0, lanes, on & 7, (on & 8) == 0


def flip(low, high, maps):
    rows, first, lanes, rows_back, first_back = maps

    def spread(x, y, rows, first):
        x = jnp.take_along_axis(x, rows, axis=0)
        y = jnp.take_along_axis(y, rows, axis=0)
        return jnp.where(first, x, y), jnp.where(first, y, x)

    low, high = spread(low, high, rows, first)
    low = jnp.take_along_axis(low, lanes[0], axis=1)
    high = jnp.take_along_axis(high, lanes[1], axis=1)
    return spread(low, high, rows_back, first_back)


def split(x):
    high = x.astype(jnp.bfloat16)
    low = (x - high.astype(jnp.float32)).astype(jnp.bfloat16)
    return high, low


def lane_nodes():
    lane = iota((8, LANES), 1)
    q = [float(v) for v in cheb_nodes(NODES)]

    def pick(t):
        return jnp.where(t < 2, jnp.where(t == 0, q[0], q[1]), jnp.where(t == 2, q[2], q[3]))

    return pick((lane >> 2) & 3), pick(lane & 3)


def position():
    at = lax.axis_index
    return at("x_hi") * 8 + at("y") * 2 + at("core"), at("z") * 2 + at("x_lo")


def iota(shape, dim):
    return lax.broadcasted_iota(jnp.int32, shape, dim)


PARTS = 8
CHUNKS = (2, 4, 4, 2, 64, LANES)


def pre_kernel(deform, coeffs, out, held, ready, first_cos, first_sin, second_cos, second_sin, sems, out_sems):
    copies = [
        pltpu.make_async_copy(
            coeffs.at[:, 0, pl.ds(2 * p, 2), 0], held.at[:, pl.ds(2 * p, 2)], sems.at[p]
        )
        for p in range(PARTS)
    ]
    sends = [
        pltpu.make_async_copy(
            ready.at[:, :, p & 3, p >> 2], out.at[:, :, p & 3, p >> 2], out_sems.at[p]
        )
        for p in range(PARTS)
    ]
    for copy in copies:
        copy.start()

    nodes = lane_nodes()
    sx, sy = [v.astype(jnp.float32) for v in position()]
    y1, y2 = warp(deform, (nodes[0] + sx) * (1 / 16), (nodes[1] + sy) * (1 / 8))
    y1, y2 = y1[0:1] * 16.0, y2[0:1] * 8.0
    first_cos[...], first_sin[...] = turn(y1 * (iota((16, LANES), 0).astype(jnp.float32) + 0.5))
    second_cos[...], second_sin[...] = turn(y2 * (iota((128, LANES), 0).astype(jnp.float32) + 0.5))
    maps = flip_maps()

    def one(b1):
        c1, s1 = first_cos[b1 : b1 + 1, :], first_sin[b1 : b1 + 1, :]
        for k in range(8):
            turned = []
            for half in range(2):
                at = pl.ds(16 * k + 8 * half, 8)
                c2, s2 = second_cos[at, :], second_sin[at, :]
                c = c1 * c2 - s1 * s2
                s = s1 * c2 + c1 * s2
                re, im = held[0, b1, at, :], held[1, b1, at, :]
                turned.append((re * c + im * s, im * c - re * s))
            for z in range(2):
                low, high = flip(turned[0][z], turned[1][z], maps)
                at = 32 * (k & 1) + 16 * z
                spot = (b1 & 1, k >> 1, (b1 >> 1) & 3, b1 >> 3)
                ready[(*spot, pl.ds(at, 8))] = low
                ready[(*spot, pl.ds(at + 8, 8))] = high

    for q in range(0, PARTS, 2):
        for p in (q, q + 1):
            copies[p].wait()
        for b1 in range(2 * q, 2 * q + 4):
            one(b1)
        for p in (q, q + 1):
            sends[p].start()
    for send in sends:
        send.wait()


def pre(coeffs, deform):
    return pl.pallas_call(
        pre_kernel,
        out_shape=jax.ShapeDtypeStruct(CHUNKS, jnp.float32),
        in_specs=[
            pl.BlockSpec(memory_space=pltpu.SMEM),
            pl.BlockSpec(memory_space=pltpu.HBM),
        ],
        out_specs=pl.BlockSpec(memory_space=pltpu.HBM),
        scratch_shapes=[
            pltpu.VMEM((2, 16, 128, LANES), jnp.float32),
            pltpu.VMEM(CHUNKS, jnp.float32),
            pltpu.VMEM((16, LANES), jnp.float32),
            pltpu.VMEM((16, LANES), jnp.float32),
            pltpu.VMEM((128, LANES), jnp.float32),
            pltpu.VMEM((128, LANES), jnp.float32),
            pltpu.SemaphoreType.DMA((PARTS,)),
            pltpu.SemaphoreType.DMA((PARTS,)),
        ],
        compiler_params=pltpu.CompilerParams(vmem_limit_bytes=60 * MIB),
        cost_estimate=pl.CostEstimate(
            flops=10 * MIB, bytes_accessed=4 * MIB, transcendentals=0
        ),
    )(deform, coeffs)


def phase_rows(tables, deform, store):
    y1, y2 = warp(deform, tables[0], tables[1])
    c, s = turn(tables[2] * y1 + tables[3] * y2)
    real = tables[4] < 0.5
    for child in range(2):
        sine_part = s if child else -s
        store[child, 0] = jnp.where(real, c, sine_part)
        store[child, 1] = jnp.where(real, -sine_part, c)


def dot(a, b):
    return jnp.dot(a, b, precision=lax.Precision.HIGHEST, preferred_element_type=jnp.float32)


def level(pattern, rows, child, part):
    shape = pattern.shape
    real = (iota(shape, 0) & POINTS) == 0
    return pattern * jnp.where(real, rows[child][0][:, part], rows[child][1][:, part])


def build_kernel(
    deform, inner, outer, wide, px, py, px_last, m1_out, m2_out, first, second, rows_in, rows_out, m1, m2, sems
):
    phase_rows(inner, deform, rows_in)
    phase_rows(outer, deform, rows_out)

    def chain(rows, at_x, at_y, at_last, keep):
        last = jnp.concatenate(
            [level(px_last[...], rows, c, slice(at_last, at_last + 64)) for c in range(2)], axis=0
        )
        parts = [dot(last, level(py[...], rows, c, slice(at_y, at_y + 128))) for c in range(2)]
        joined = jnp.concatenate(
            [parts[cy][32 * cx : 32 * cx + keep] for cx in range(2) for cy in range(2)], axis=0
        )
        return [
            dot(joined, level(px[...], rows, c, slice(at_x, at_x + 256))) for c in range(2)
        ]

    def group(g, carry):
        rows = [[rows_in[c, z, pl.ds(g, 1), :] for z in range(2)] for c in range(2)]
        for c, value in enumerate(chain(rows, 0, 256, 384, 16)):
            high, low = split(value)
            m1[g, pl.ds(64 * c, 64), :] = high
            m1[g, pl.ds(128 + 64 * c, 64), :] = low
        return carry

    lax.fori_loop(0, 16, group, 0)
    copies = [
        pltpu.make_async_copy(m1, m1_out, sems.at[0]),
        pltpu.make_async_copy(m2, m2_out, sems.at[1]),
    ]
    copies[0].start()

    rows = [[rows_out[c, z, 0:1, :] for z in range(2)] for c in range(2)]
    for c5, value in enumerate(chain(rows, 512, 768, 896, 32)):
        for c4 in range(2):
            block = dot(value, level(wide[...], rows, c4, slice(0, 512)))
            for c7 in range(2):
                for c6 in range(2):
                    high, low = split(block[64 * c7 + 32 * c6 : 64 * c7 + 32 * c6 + 32])
                    at = 32 * (8 * c5 + 4 * c7 + 2 * c4 + c6)
                    m2[0, pl.ds(at, 32), :] = high
                    m2[1, pl.ds(at, 32), :] = low

    copies[1].start()
    sx, sy = [v.astype(jnp.float32) for v in position()]
    y1, y2 = warp(deform, *lane_nodes())
    c, s = turn(y1[0:1] * (iota((16, LANES), 0).astype(jnp.float32) + (16.0 * sx + 0.5)))
    scale = math.sqrt(0.5) ** 7
    first[0] = c * scale
    first[1] = s * scale
    c, s = turn(y2[0:1] * (iota((128, LANES), 0).astype(jnp.float32) + (128.0 * sy + 0.5)))
    second[0] = c
    second[1] = s
    for copy in copies:
        copy.wait()


def build(deform):
    inner, outer = column_tables()
    consts = [inner, outer, pattern_y_first(), pattern_x(), pattern_y(), pattern_x_last()]
    vmem = pl.BlockSpec(memory_space=pltpu.VMEM)
    return pl.pallas_call(
        build_kernel,
        out_shape=[
            pltpu.HBM((16, 256, 256), jnp.bfloat16),
            pltpu.HBM((2, 512, 512), jnp.bfloat16),
            jax.ShapeDtypeStruct((2, 16, LANES), jnp.float32),
            jax.ShapeDtypeStruct((2, 128, LANES), jnp.float32),
        ],
        in_specs=[pl.BlockSpec(memory_space=pltpu.SMEM)] + [vmem] * 6,
        out_specs=[pl.BlockSpec(memory_space=pltpu.HBM)] * 2 + [vmem] * 2,
        scratch_shapes=[
            pltpu.VMEM((2, 2, 16, 512), jnp.float32),
            pltpu.VMEM((2, 2, 8, 1024), jnp.float32),
            pltpu.VMEM((16, 256, 256), jnp.bfloat16),
            pltpu.VMEM((2, 512, 512), jnp.bfloat16),
            pltpu.SemaphoreType.DMA((2,)),
        ],
        compiler_params=pltpu.CompilerParams(vmem_limit_bytes=16 * MIB),
        cost_estimate=pl.CostEstimate(
            flops=6000 * MIB, bytes_accessed=40 * MIB, transcendentals=0
        ),
    )(deform, *[jnp.asarray(c, dtype=jnp.float32) for c in consts])


def mul(a, b):
    return jnp.dot(a, b, preferred_element_type=jnp.float32)


def post_kernel(
    m1_in, m2_in, first, second, got, out, m1, m2, x_high, x_low, high, low, acc, done, cos, sin, sems, in_sems
):
    loads = [
        pltpu.make_async_copy(m1_in.at[pl.ds(8 * p, 8)], m1.at[pl.ds(8 * p, 8)], in_sems.at[p])
        for p in range(2)
    ] + [pltpu.make_async_copy(m2_in, m2, in_sems.at[2])]
    for load in loads:
        load.start()

    def prepare(g):
        gx, gy = g >> 2, g & 3
        x = [[], []]
        for i in range(4):
            chunk = (i & 1) * 64 + gy * 16 + ((gx & 1) * 2 + (i >> 1)) * 4 + (gx >> 1) * 2
            for j in range(2):
                re, im = got[chunk + j, 0:16, :], got[chunk + j, 16:32, :]
                x[0] += [re, im]
                x[1] += [im, -re]
        x = jnp.concatenate([jnp.concatenate(v, axis=0) for v in x], axis=1)
        x_high[g], x_low[g] = split(x)

    def stage_one(g):
        both = mul(m1[g], x_high[g])
        yh, yl = split(both[:128] + (mul(m1[g, 0:128], x_low[g]) + both[128:]))
        for z in range(2):
            at = pl.ds(32 * g + 16 * z, 16)
            for c13 in range(4):
                for c2 in range(2):
                    rows = slice(32 * c13 + 16 * c2, 32 * c13 + 16 * c2 + 16)
                    lanes = slice(128 * z, 128 * z + 128)
                    high[c13, at, pl.ds(128 * c2, 128)] = yh[rows, lanes]
                    low[c13, at, pl.ds(128 * c2, 128)] = yl[rows, lanes]

    for g in range(16):
        prepare(g)
    for p in range(2):
        loads[p].wait()
        for g in range(8 * p, 8 * p + 8):
            stage_one(g)
    loads[2].wait()

    maps = flip_maps()

    def copies(c13):
        return [
            pltpu.make_async_copy(
                done.at[z, pl.ds(4 * c13, 4)], out.at[z, pl.ds(4 * c13, 4)], sems.at[z, c13]
            )
            for z in range(2)
        ]

    for c13 in range(4):
        acc[...] = mul(m2[0], high[c13]) + (mul(m2[0], low[c13]) + mul(m2[1], high[c13]))

        def finish(c57, carry):
            cx = 4 * c13 + c57
            c1, s1 = first[0, pl.ds(cx, 1), :], first[1, pl.ds(cx, 1), :]
            c2, s2 = second[0], second[1]
            c = c1 * c2 - s1 * s2
            s = s1 * c2 + c1 * s2
            cos[...] = c
            sin[...] = s
            for cy in range(8):
                at = pl.multiple_of(128 * c57, 128) + 32 * (cy & 3)
                part = pl.ds(128 * (cy >> 2), 128)
                re, im = [
                    flip(
                        acc[pl.ds(at + 16 * z, 8), part],
                        acc[pl.ds(at + 16 * z + 8, 8), part],
                        maps,
                    )
                    for z in range(2)
                ]
                for half in range(2):
                    rows = pl.ds(64 * half + cy, 8, stride=8)
                    c, s = cos[rows, :], sin[rows, :]
                    done[0, cx, rows, :] = re[half] * c - im[half] * s
                    done[1, cx, rows, :] = im[half] * c + re[half] * s
            return carry

        lax.fori_loop(0, 4, finish, 0, unroll=4)
        for copy in copies(c13):
            copy.start()
    for c13 in range(4):
        for copy in copies(c13):
            copy.wait()


def post(m1, m2, first, second, got):
    vmem = pl.BlockSpec(memory_space=pltpu.VMEM)
    return pl.pallas_call(
        post_kernel,
        out_shape=jax.ShapeDtypeStruct((2, 16, 128, LANES), jnp.float32),
        in_specs=[pl.BlockSpec(memory_space=pltpu.HBM)] * 2 + [vmem] * 3,
        out_specs=pl.BlockSpec(memory_space=pltpu.HBM),
        scratch_shapes=[
            pltpu.VMEM((16, 256, 256), jnp.bfloat16),
            pltpu.VMEM((2, 512, 512), jnp.bfloat16),
            pltpu.VMEM((16, 256, 256), jnp.bfloat16),
            pltpu.VMEM((16, 256, 256), jnp.bfloat16),
            pltpu.VMEM((4, 512, 256), jnp.bfloat16),
            pltpu.VMEM((4, 512, 256), jnp.bfloat16),
            pltpu.VMEM((512, 256), jnp.float32),
            pltpu.VMEM((2, 16, 128, LANES), jnp.float32),
            pltpu.VMEM((128, LANES), jnp.float32),
            pltpu.VMEM((128, LANES), jnp.float32),
            pltpu.SemaphoreType.DMA((2, 4)),
            pltpu.SemaphoreType.DMA((3,)),
        ],
        compiler_params=pltpu.CompilerParams(vmem_limit_bytes=16 * MIB),
        cost_estimate=pl.CostEstimate(
            flops=4000 * MIB, bytes_accessed=10 * MIB, transcendentals=0
        ),
    )(
        *[pltpu.with_memory_space_constraint(m, pltpu.HBM) for m in (m1, m2)],
        first,
        second,
        got,
    )


def body(coeffs, deform):
    sent = pre(coeffs, deform)
    sent = sent.reshape(128, 32, LANES)
    got = lax.all_to_all(sent, ("core", "z", "y", "x_hi", "x_lo"), 0, 0, tiled=True)
    return post(*build(deform), got)


def solution(mesh):
    fine = Mesh(mesh.devices.reshape(2, 4, 2, 4, 2), ("x_hi", "y", "core", "z", "x_lo"))
    sx, sy = ("x_hi", "y", "core"), ("z", "x_lo")
    return jax.shard_map(
        body,
        mesh=fine,
        in_specs=(P(None, sx, None, sy, None, None), P()),
        out_specs=P(None, sx, sy, None),
        check_vma=False,
    )
```

```python
import math

import jax
import jax.numpy as jnp
import numpy as np
from jax import lax
from jax.experimental import pallas as pl
from jax.experimental.pallas import tpu as pltpu
from jax.sharding import Mesh
from jax.sharding import PartitionSpec as P

NODES = 4
RHS = 8
POINTS = NODES * NODES
LANES = RHS * POINTS
MIB = 1 << 20


def cheb_nodes(count):
    return (1.0 - np.cos(np.pi * (2.0 * np.arange(count) + 1.0) / (2.0 * count))) / 2.0


def lagrange_table(count):
    nodes = cheb_nodes(count)
    table = np.ones((count, 2, count))
    for row in range(count):
        for sibling in range(2):
            spots = (sibling + nodes) / 2.0
            for other in range(count):
                if other != row:
                    table[row, sibling] *= (spots - nodes[other]) / (nodes[row] - nodes[other])
    return table


def pattern_x():
    L, e2, e4, one = lagrange_table(NODES), np.eye(2), np.eye(NODES), np.ones((2, 2))
    return np.einsum("hH,yY,zZ,asu,vV->hyzavHsYZuV", e2, e2, one, L, e4).reshape(128, 256)


def pattern_y():
    L, e2, e4, one = lagrange_table(NODES), np.eye(2), np.eye(NODES), np.ones((2, 2))
    return np.einsum("hH,zZ,aA,bsv->hzabHsZAv", e2, one, e4, L).reshape(64, 128)


def pattern_x_last():
    L, e4, one = lagrange_table(NODES), np.eye(NODES), np.ones((2, 2))
    return np.einsum("zZ,asu,bB->zabsZuB", one, L, e4).reshape(32, 64)


def pattern_y_first():
    L, e2, e4, one = lagrange_table(NODES), np.eye(2), np.eye(NODES), np.ones((2, 2))
    return np.einsum("gG,hH,zZ,uU,bsv->ghzubGHsZUv", e4, e2, one, e4, L).reshape(256, 512)


def columns(dims, first, second, first_turns, second_turns):
    names, sizes = zip(*dims)
    grid = dict(zip(names, np.meshgrid(*[np.arange(s) for s in sizes], indexing="ij")))
    shape = grid["z"].shape
    flat = lambda v: np.broadcast_to(v, shape).reshape(-1)
    return np.stack(
        [flat(first(grid)), flat(second(grid)), flat(first_turns), flat(second_turns), flat(grid["z"])]
    )


def column_tables():
    q = cheb_nodes(NODES)
    groups = []
    for gx in range(4):
        for gy in range(4):
            one = columns(
                [("h", 2), ("l", 2), ("y", 2), ("z", 2), ("u", 4), ("v", 4)],
                lambda g: (4 * gx + 2 * g["h"] + g["l"] + q[g["u"]]) / 16,
                lambda g: (2 * gy + g["y"] + q[g["v"]]) / 8,
                4.0,
                0.0,
            )
            two = columns(
                [("h", 2), ("y", 2), ("z", 2), ("u", 4), ("v", 4)],
                lambda g: (2 * gx + g["h"] + q[g["u"]]) / 8,
                lambda g: (2 * gy + g["y"] + q[g["v"]]) / 8,
                0.0,
                2.0,
            )
            three = columns(
                [("h", 2), ("z", 2), ("u", 4), ("v", 4)],
                lambda g: (2 * gx + g["h"] + q[g["u"]]) / 8,
                lambda g: (gy + q[g["v"]]) / 4,
                2.0,
                0.0,
            )
            groups.append(np.concatenate([one, two, three, np.zeros((5, 64))], axis=1))
    inner = np.stack(groups, axis=1)
    four = columns(
        [("g", 4), ("h", 2), ("l", 2), ("z", 2), ("u", 4), ("v", 4)],
        lambda g: (g["g"] + q[g["u"]]) / 4,
        lambda g: (2 * g["h"] + g["l"] + q[g["v"]]) / 4,
        0.0,
        1.0,
    )
    five = columns(
        [("h", 2), ("l", 2), ("y", 2), ("z", 2), ("u", 4), ("v", 4)],
        lambda g: (2 * g["h"] + g["l"] + q[g["u"]]) / 4,
        lambda g: (g["y"] + q[g["v"]]) / 2,
        1.0,
        0.0,
    )
    six = columns(
        [("h", 2), ("y", 2), ("z", 2), ("u", 4), ("v", 4)],
        lambda g: (g["h"] + q[g["u"]]) / 2,
        lambda g: (g["y"] + q[g["v"]]) / 2,
        0.0,
        0.5,
    )
    seven = columns(
        [("h", 2), ("z", 2), ("u", 4), ("v", 4)],
        lambda g: (g["h"] + q[g["u"]]) / 2,
        lambda g: q[g["v"]] + 0.0 * g["h"],
        0.5,
        0.0,
    )
    outer = np.concatenate([four, five, six, seven, np.zeros((5, 64))], axis=1)
    outer = np.broadcast_to(outer[:, None], (5, 8, 1024))
    return inner.astype(np.float32), outer.astype(np.float32)


SINE = [
    (-1) ** k * (2.0 * math.pi) ** (2 * k + 1) / math.factorial(2 * k + 1) for k in range(7)
]


def sine_quarter(x):
    square = x * x
    total = jnp.full_like(x, SINE[-1])
    for coefficient in SINE[-2::-1]:
        total = total * square + coefficient
    return total * x


def turn(x):
    part = x - jnp.round(x)
    size = jnp.abs(part)
    folded = jnp.where(size > 0.25, jnp.where(part > 0, 0.5, -0.5) - part, part)
    return sine_quarter(0.25 - size), sine_quarter(folded)


def sine(x):
    part = x - jnp.round(x)
    folded = jnp.where(jnp.abs(part) > 0.25, jnp.where(part > 0, 0.5, -0.5) - part, part)
    return sine_quarter(folded)


def warp(deform, first, second):
    total, differ = 0.5 * (first + second), 0.5 * (first - second)
    y1, y2 = None, None
    for m in range(4):
        one = deform[0, m] * sine(total * (m + 1.0))
        two = deform[1, m] * sine(differ * (m + 1.0))
        y1 = one if y1 is None else y1 + one
        y2 = two if y2 is None else y2 + two
    return first + y1, second + y2


def flip_maps():
    row, lane = iota((8, LANES), 0), iota((8, LANES), 1)
    spot = lane & 15
    back, on = row - spot, row + spot
    lanes = [(lane & ~15) | ((back + 8 * half) & 15) for half in range(2)]
    return back & 7, (back & 8) == 0, lanes, on & 7, (on & 8) == 0


def flip(low, high, maps):
    rows, first, lanes, rows_back, first_back = maps

    def spread(x, y, rows, first):
        x = jnp.take_along_axis(x, rows, axis=0)
        y = jnp.take_along_axis(y, rows, axis=0)
        return jnp.where(first, x, y), jnp.where(first, y, x)

    low, high = spread(low, high, rows, first)
    low = jnp.take_along_axis(low, lanes[0], axis=1)
    high = jnp.take_along_axis(high, lanes[1], axis=1)
    return spread(low, high, rows_back, first_back)


def split(x):
    high = x.astype(jnp.bfloat16)
    low = (x - high.astype(jnp.float32)).astype(jnp.bfloat16)
    return high, low


def lane_nodes():
    lane = iota((8, LANES), 1)
    q = [float(v) for v in cheb_nodes(NODES)]

    def pick(t):
        return jnp.where(t < 2, jnp.where(t == 0, q[0], q[1]), jnp.where(t == 2, q[2], q[3]))

    return pick((lane >> 2) & 3), pick(lane & 3)


def position():
    at = lax.axis_index
    return at("x_hi") * 8 + at("y") * 2 + at("core"), at("z") * 2 + at("x_lo")


def iota(shape, dim):
    return lax.broadcasted_iota(jnp.int32, shape, dim)


PARTS = 8
CHUNKS = (2, 4, 4, 2, 64, LANES)


def pre_kernel(deform, coeffs, out, held, ready, first_cos, first_sin, second_cos, second_sin, sems, out_sems):
    copies = [
        pltpu.make_async_copy(
            coeffs.at[:, 0, pl.ds(2 * p, 2), 0], held.at[:, pl.ds(2 * p, 2)], sems.at[p]
        )
        for p in range(PARTS)
    ]
    sends = [
        pltpu.make_async_copy(
            ready.at[:, :, p & 3, p >> 2], out.at[:, :, p & 3, p >> 2], out_sems.at[p]
        )
        for p in range(PARTS)
    ]
    for copy in copies:
        copy.start()

    nodes = lane_nodes()
    sx, sy = [v.astype(jnp.float32) for v in position()]
    y1, y2 = warp(deform, (nodes[0] + sx) * (1 / 16), (nodes[1] + sy) * (1 / 8))
    y1, y2 = y1[0:1] * 16.0, y2[0:1] * 8.0
    first_cos[...], first_sin[...] = turn(y1 * (iota((16, LANES), 0).astype(jnp.float32) + 0.5))
    second_cos[...], second_sin[...] = turn(y2 * (iota((128, LANES), 0).astype(jnp.float32) + 0.5))
    maps = flip_maps()

    def one(b1):
        c1, s1 = first_cos[b1 : b1 + 1, :], first_sin[b1 : b1 + 1, :]
        for k in range(8):
            turned = []
            for half in range(2):
                at = pl.ds(16 * k + 8 * half, 8)
                c2, s2 = second_cos[at, :], second_sin[at, :]
                c = c1 * c2 - s1 * s2
                s = s1 * c2 + c1 * s2
                re, im = held[0, b1, at, :], held[1, b1, at, :]
                turned.append((re * c + im * s, im * c - re * s))
            for z in range(2):
                low, high = flip(turned[0][z], turned[1][z], maps)
                at = 32 * (k & 1) + 16 * z
                spot = (b1 & 1, k >> 1, (b1 >> 1) & 3, b1 >> 3)
                ready[(*spot, pl.ds(at, 8))] = low
                ready[(*spot, pl.ds(at + 8, 8))] = high

    for q in range(0, PARTS, 2):
        for p in (q, q + 1):
            copies[p].wait()
        for b1 in range(2 * q, 2 * q + 4):
            one(b1)
        for p in (q, q + 1):
            sends[p].start()
    for send in sends:
        send.wait()


def pre(coeffs, deform):
    return pl.pallas_call(
        pre_kernel,
        out_shape=jax.ShapeDtypeStruct(CHUNKS, jnp.float32),
        in_specs=[
            pl.BlockSpec(memory_space=pltpu.SMEM),
            pl.BlockSpec(memory_space=pltpu.HBM),
        ],
        out_specs=pl.BlockSpec(memory_space=pltpu.HBM),
        scratch_shapes=[
            pltpu.VMEM((2, 16, 128, LANES), jnp.float32),
            pltpu.VMEM(CHUNKS, jnp.float32),
            pltpu.VMEM((16, LANES), jnp.float32),
            pltpu.VMEM((16, LANES), jnp.float32),
            pltpu.VMEM((128, LANES), jnp.float32),
            pltpu.VMEM((128, LANES), jnp.float32),
            pltpu.SemaphoreType.DMA((PARTS,)),
            pltpu.SemaphoreType.DMA((PARTS,)),
        ],
        compiler_params=pltpu.CompilerParams(vmem_limit_bytes=60 * MIB),
        cost_estimate=pl.CostEstimate(
            flops=10 * MIB, bytes_accessed=4 * MIB, transcendentals=0
        ),
    )(deform, coeffs)


def phase_rows(tables, deform, store):
    y1, y2 = warp(deform, tables[0], tables[1])
    c, s = turn(tables[2] * y1 + tables[3] * y2)
    real = tables[4] < 0.5
    for child in range(2):
        sine_part = s if child else -s
        store[child, 0] = jnp.where(real, c, sine_part)
        store[child, 1] = jnp.where(real, -sine_part, c)


def dot(a, b):
    return jnp.dot(a, b, precision=lax.Precision.HIGHEST, preferred_element_type=jnp.float32)


def level(pattern, rows, child, part):
    shape = pattern.shape
    real = (iota(shape, 0) & POINTS) == 0
    return pattern * jnp.where(real, rows[child][0][:, part], rows[child][1][:, part])


def build_kernel(
    deform, inner, outer, wide, px, py, px_last, m1_out, m2_out, first, second, rows_in, rows_out, m1, m2, sems
):
    phase_rows(inner, deform, rows_in)
    phase_rows(outer, deform, rows_out)

    def chain(rows, at_x, at_y, at_last, keep):
        last = jnp.concatenate(
            [level(px_last[...], rows, c, slice(at_last, at_last + 64)) for c in range(2)], axis=0
        )
        parts = [dot(last, level(py[...], rows, c, slice(at_y, at_y + 128))) for c in range(2)]
        joined = jnp.concatenate(
            [parts[cy][32 * cx : 32 * cx + keep] for cx in range(2) for cy in range(2)], axis=0
        )
        return [
            dot(joined, level(px[...], rows, c, slice(at_x, at_x + 256))) for c in range(2)
        ]

    def group(g, carry):
        rows = [[rows_in[c, z, pl.ds(g, 1), :] for z in range(2)] for c in range(2)]
        for c, value in enumerate(chain(rows, 0, 256, 384, 16)):
            high, low = split(value)
            m1[g, pl.ds(64 * c, 64), :] = high
            m1[g, pl.ds(128 + 64 * c, 64), :] = low
        return carry

    lax.fori_loop(0, 16, group, 0)
    copies = [
        pltpu.make_async_copy(m1, m1_out, sems.at[0]),
        pltpu.make_async_copy(m2, m2_out, sems.at[1]),
    ]
    copies[0].start()

    rows = [[rows_out[c, z, 0:1, :] for z in range(2)] for c in range(2)]
    for c5, value in enumerate(chain(rows, 512, 768, 896, 32)):
        for c4 in range(2):
            block = dot(value, level(wide[...], rows, c4, slice(0, 512)))
            for c7 in range(2):
                for c6 in range(2):
                    high, low = split(block[64 * c7 + 32 * c6 : 64 * c7 + 32 * c6 + 32])
                    at = 32 * (8 * c5 + 4 * c7 + 2 * c4 + c6)
                    m2[0, pl.ds(at, 32), :] = high
                    m2[1, pl.ds(at, 32), :] = low

    copies[1].start()
    sx, sy = [v.astype(jnp.float32) for v in position()]
    y1, y2 = warp(deform, *lane_nodes())
    c, s = turn(y1[0:1] * (iota((16, LANES), 0).astype(jnp.float32) + (16.0 * sx + 0.5)))
    scale = math.sqrt(0.5) ** 7
    first[0] = c * scale
    first[1] = s * scale
    c, s = turn(y2[0:1] * (iota((128, LANES), 0).astype(jnp.float32) + (128.0 * sy + 0.5)))
    second[0] = c
    second[1] = s
    for copy in copies:
        copy.wait()


def build(deform):
    inner, outer = column_tables()
    consts = [inner, outer, pattern_y_first(), pattern_x(), pattern_y(), pattern_x_last()]
    vmem = pl.BlockSpec(memory_space=pltpu.VMEM)
    return pl.pallas_call(
        build_kernel,
        out_shape=[
            pltpu.HBM((16, 256, 256), jnp.bfloat16),
            pltpu.HBM((2, 512, 512), jnp.bfloat16),
            jax.ShapeDtypeStruct((2, 16, LANES), jnp.float32),
            jax.ShapeDtypeStruct((2, 128, LANES), jnp.float32),
        ],
        in_specs=[pl.BlockSpec(memory_space=pltpu.SMEM)] + [vmem] * 6,
        out_specs=[pl.BlockSpec(memory_space=pltpu.HBM)] * 2 + [vmem] * 2,
        scratch_shapes=[
            pltpu.VMEM((2, 2, 16, 512), jnp.float32),
            pltpu.VMEM((2, 2, 8, 1024), jnp.float32),
            pltpu.VMEM((16, 256, 256), jnp.bfloat16),
            pltpu.VMEM((2, 512, 512), jnp.bfloat16),
            pltpu.SemaphoreType.DMA((2,)),
        ],
        compiler_params=pltpu.CompilerParams(vmem_limit_bytes=16 * MIB),
        cost_estimate=pl.CostEstimate(
            flops=6000 * MIB, bytes_accessed=40 * MIB, transcendentals=0
        ),
    )(deform, *[jnp.asarray(c, dtype=jnp.float32) for c in consts])


def mul(a, b):
    return jnp.dot(a, b, preferred_element_type=jnp.float32)


LOADS = ((0, 4), (4, 16))


def post_kernel(
    m1_in, m2_in, first, second, got, out, m1, m2, x_high, x_low, high, low, acc, done, sems, in_sems
):
    loads = [
        pltpu.make_async_copy(m1_in.at[pl.ds(a, b - a)], m1.at[pl.ds(a, b - a)], in_sems.at[p])
        for p, (a, b) in enumerate(LOADS)
    ] + [pltpu.make_async_copy(m2_in, m2, in_sems.at[2])]
    for load in loads:
        load.start()

    def prepare(g):
        gx, gy = g >> 2, g & 3
        x = [[], []]
        for i in range(4):
            chunk = (i & 1) * 64 + gy * 16 + ((gx & 1) * 2 + (i >> 1)) * 4 + (gx >> 1) * 2
            for j in range(2):
                re, im = got[chunk + j, 0:16, :], got[chunk + j, 16:32, :]
                x[0] += [re, im]
                x[1] += [im, -re]
        x = jnp.concatenate([jnp.concatenate(v, axis=0) for v in x], axis=1)
        x_high[g], x_low[g] = split(x)

    def stage_one(g):
        both = mul(m1[g], x_high[g])
        yh, yl = split(both[:128] + (mul(m1[g, 0:128], x_low[g]) + both[128:]))
        for z in range(2):
            at = pl.ds(32 * g + 16 * z, 16)
            for c13 in range(4):
                for c2 in range(2):
                    rows = slice(32 * c13 + 16 * c2, 32 * c13 + 16 * c2 + 16)
                    lanes = slice(128 * z, 128 * z + 128)
                    high[c13, at, pl.ds(128 * c2, 128)] = yh[rows, lanes]
                    low[c13, at, pl.ds(128 * c2, 128)] = yl[rows, lanes]

    for g in range(16):
        prepare(g)
    for p, (a, b) in enumerate(LOADS):
        loads[p].wait()
        for g in range(a, b):
            stage_one(g)
    loads[2].wait()

    maps = flip_maps()

    def copies(c13):
        return [
            pltpu.make_async_copy(
                done.at[z, pl.ds(4 * c13, 4)], out.at[z, pl.ds(4 * c13, 4)], sems.at[z, c13]
            )
            for z in range(2)
        ]

    for c13 in range(4):
        acc[...] = mul(m2[0], high[c13]) + (mul(m2[0], low[c13]) + mul(m2[1], high[c13]))

        def finish(c57, carry):
            cx = 4 * c13 + c57
            c1, s1 = first[0, pl.ds(cx, 1), :], first[1, pl.ds(cx, 1), :]
            for cy in range(8):
                at = pl.multiple_of(128 * c57, 128) + 32 * (cy & 3)
                part = pl.ds(128 * (cy >> 2), 128)
                re, im = [
                    flip(
                        acc[pl.ds(at + 16 * z, 8), part],
                        acc[pl.ds(at + 16 * z + 8, 8), part],
                        maps,
                    )
                    for z in range(2)
                ]
                for half in range(2):
                    rows = pl.ds(64 * half + cy, 8, stride=8)
                    c2, s2 = second[0, rows, :], second[1, rows, :]
                    c, s = c1 * c2 - s1 * s2, s1 * c2 + c1 * s2
                    done[0, cx, rows, :] = re[half] * c - im[half] * s
                    done[1, cx, rows, :] = im[half] * c + re[half] * s
            return carry

        lax.fori_loop(0, 4, finish, 0, unroll=4)
        for copy in copies(c13):
            copy.start()
    for c13 in range(4):
        for copy in copies(c13):
            copy.wait()


def post(m1, m2, first, second, got):
    vmem = pl.BlockSpec(memory_space=pltpu.VMEM)
    return pl.pallas_call(
        post_kernel,
        out_shape=jax.ShapeDtypeStruct((2, 16, 128, LANES), jnp.float32),
        in_specs=[pl.BlockSpec(memory_space=pltpu.HBM)] * 2 + [vmem] * 3,
        out_specs=pl.BlockSpec(memory_space=pltpu.HBM),
        scratch_shapes=[
            pltpu.VMEM((16, 256, 256), jnp.bfloat16),
            pltpu.VMEM((2, 512, 512), jnp.bfloat16),
            pltpu.VMEM((16, 256, 256), jnp.bfloat16),
            pltpu.VMEM((16, 256, 256), jnp.bfloat16),
            pltpu.VMEM((4, 512, 256), jnp.bfloat16),
            pltpu.VMEM((4, 512, 256), jnp.bfloat16),
            pltpu.VMEM((512, 256), jnp.float32),
            pltpu.VMEM((2, 16, 128, LANES), jnp.float32),
            pltpu.SemaphoreType.DMA((2, 4)),
            pltpu.SemaphoreType.DMA((3,)),
        ],
        compiler_params=pltpu.CompilerParams(vmem_limit_bytes=16 * MIB),
        cost_estimate=pl.CostEstimate(
            flops=4000 * MIB, bytes_accessed=10 * MIB, transcendentals=0
        ),
    )(
        *[pltpu.with_memory_space_constraint(m, pltpu.HBM) for m in (m1, m2)],
        first,
        second,
        got,
    )


def body(coeffs, deform):
    sent = pre(coeffs, deform)
    sent = sent.reshape(128, 32, LANES)
    got = lax.all_to_all(sent, ("core", "z", "y", "x_hi", "x_lo"), 0, 0, tiled=True)
    return post(*build(deform), got)


def solution(mesh):
    fine = Mesh(mesh.devices.reshape(2, 4, 2, 4, 2), ("x_hi", "y", "core", "z", "x_lo"))
    sx, sy = ("x_hi", "y", "core"), ("z", "x_lo")
    return jax.shard_map(
        body,
        mesh=fine,
        in_specs=(P(None, sx, None, sy, None, None), P()),
        out_specs=P(None, sx, sy, None),
        check_vma=False,
    )
```

```python
import math

import jax
import jax.numpy as jnp
import numpy as np
from jax import lax
from jax.experimental import pallas as pl
from jax.experimental.pallas import tpu as pltpu
from jax.sharding import Mesh
from jax.sharding import PartitionSpec as P

NODES = 4
RHS = 8
POINTS = NODES * NODES
LANES = RHS * POINTS
MIB = 1 << 20


def cheb_nodes(count):
    return (1.0 - np.cos(np.pi * (2.0 * np.arange(count) + 1.0) / (2.0 * count))) / 2.0


def lagrange_table(count):
    nodes = cheb_nodes(count)
    table = np.ones((count, 2, count))
    for row in range(count):
        for sibling in range(2):
            spots = (sibling + nodes) / 2.0
            for other in range(count):
                if other != row:
                    table[row, sibling] *= (spots - nodes[other]) / (nodes[row] - nodes[other])
    return table


def pattern_x():
    L, e2, e4, one = lagrange_table(NODES), np.eye(2), np.eye(NODES), np.ones((2, 2))
    return np.einsum("hH,yY,zZ,asu,vV->hyzavHsYZuV", e2, e2, one, L, e4).reshape(128, 256)


def pattern_y():
    L, e2, e4, one = lagrange_table(NODES), np.eye(2), np.eye(NODES), np.ones((2, 2))
    return np.einsum("hH,zZ,aA,bsv->hzabHsZAv", e2, one, e4, L).reshape(64, 128)


def pattern_x_last():
    L, e4, one = lagrange_table(NODES), np.eye(NODES), np.ones((2, 2))
    return np.einsum("zZ,asu,bB->zabsZuB", one, L, e4).reshape(32, 64)


def pattern_y_first():
    L, e2, e4, one = lagrange_table(NODES), np.eye(2), np.eye(NODES), np.ones((2, 2))
    return np.einsum("gG,hH,zZ,uU,bsv->ghzubGHsZUv", e4, e2, one, e4, L).reshape(256, 512)


def columns(dims, first, second, first_turns, second_turns):
    names, sizes = zip(*dims)
    grid = dict(zip(names, np.meshgrid(*[np.arange(s) for s in sizes], indexing="ij")))
    shape = grid["z"].shape
    flat = lambda v: np.broadcast_to(v, shape).reshape(-1)
    return np.stack(
        [flat(first(grid)), flat(second(grid)), flat(first_turns), flat(second_turns), flat(grid["z"])]
    )


def column_tables():
    q = cheb_nodes(NODES)
    groups = []
    for gx in range(4):
        for gy in range(4):
            one = columns(
                [("h", 2), ("l", 2), ("y", 2), ("z", 2), ("u", 4), ("v", 4)],
                lambda g: (4 * gx + 2 * g["h"] + g["l"] + q[g["u"]]) / 16,
                lambda g: (2 * gy + g["y"] + q[g["v"]]) / 8,
                4.0,
                0.0,
            )
            two = columns(
                [("h", 2), ("y", 2), ("z", 2), ("u", 4), ("v", 4)],
                lambda g: (2 * gx + g["h"] + q[g["u"]]) / 8,
                lambda g: (2 * gy + g["y"] + q[g["v"]]) / 8,
                0.0,
                2.0,
            )
            three = columns(
                [("h", 2), ("z", 2), ("u", 4), ("v", 4)],
                lambda g: (2 * gx + g["h"] + q[g["u"]]) / 8,
                lambda g: (gy + q[g["v"]]) / 4,
                2.0,
                0.0,
            )
            groups.append(np.concatenate([one, two, three, np.zeros((5, 64))], axis=1))
    inner = np.stack(groups, axis=1)
    four = columns(
        [("g", 4), ("h", 2), ("l", 2), ("z", 2), ("u", 4), ("v", 4)],
        lambda g: (g["g"] + q[g["u"]]) / 4,
        lambda g: (2 * g["h"] + g["l"] + q[g["v"]]) / 4,
        0.0,
        1.0,
    )
    five = columns(
        [("h", 2), ("l", 2), ("y", 2), ("z", 2), ("u", 4), ("v", 4)],
        lambda g: (2 * g["h"] + g["l"] + q[g["u"]]) / 4,
        lambda g: (g["y"] + q[g["v"]]) / 2,
        1.0,
        0.0,
    )
    six = columns(
        [("h", 2), ("y", 2), ("z", 2), ("u", 4), ("v", 4)],
        lambda g: (g["h"] + q[g["u"]]) / 2,
        lambda g: (g["y"] + q[g["v"]]) / 2,
        0.0,
        0.5,
    )
    seven = columns(
        [("h", 2), ("z", 2), ("u", 4), ("v", 4)],
        lambda g: (g["h"] + q[g["u"]]) / 2,
        lambda g: q[g["v"]] + 0.0 * g["h"],
        0.5,
        0.0,
    )
    outer = np.concatenate([four, five, six, seven, np.zeros((5, 64))], axis=1)
    outer = np.broadcast_to(outer[:, None], (5, 8, 1024))
    return inner.astype(np.float32), outer.astype(np.float32)


SINE = [
    (-1) ** k * (2.0 * math.pi) ** (2 * k + 1) / math.factorial(2 * k + 1) for k in range(7)
]


def sine_quarter(x):
    square = x * x
    total = jnp.full_like(x, SINE[-1])
    for coefficient in SINE[-2::-1]:
        total = total * square + coefficient
    return total * x


def turn(x):
    part = x - jnp.round(x)
    size = jnp.abs(part)
    folded = jnp.where(size > 0.25, jnp.where(part > 0, 0.5, -0.5) - part, part)
    return sine_quarter(0.25 - size), sine_quarter(folded)


def sine(x):
    part = x - jnp.round(x)
    folded = jnp.where(jnp.abs(part) > 0.25, jnp.where(part > 0, 0.5, -0.5) - part, part)
    return sine_quarter(folded)


def warp(deform, first, second):
    total, differ = 0.5 * (first + second), 0.5 * (first - second)
    y1, y2 = None, None
    for m in range(4):
        one = deform[0, m] * sine(total * (m + 1.0))
        two = deform[1, m] * sine(differ * (m + 1.0))
        y1 = one if y1 is None else y1 + one
        y2 = two if y2 is None else y2 + two
    return first + y1, second + y2


def flip_maps():
    row, lane = iota((8, LANES), 0), iota((8, LANES), 1)
    spot = lane & 15
    back, on = row - spot, row + spot
    lanes = [(lane & ~15) | ((back + 8 * half) & 15) for half in range(2)]
    return back & 7, (back & 8) == 0, lanes, on & 7, (on & 8) == 0


def flip(low, high, maps):
    rows, first, lanes, rows_back, first_back = maps

    def spread(x, y, rows, first):
        x = jnp.take_along_axis(x, rows, axis=0)
        y = jnp.take_along_axis(y, rows, axis=0)
        return jnp.where(first, x, y), jnp.where(first, y, x)

    low, high = spread(low, high, rows, first)
    low = jnp.take_along_axis(low, lanes[0], axis=1)
    high = jnp.take_along_axis(high, lanes[1], axis=1)
    return spread(low, high, rows_back, first_back)


def split(x):
    high = x.astype(jnp.bfloat16)
    low = (x - high.astype(jnp.float32)).astype(jnp.bfloat16)
    return high, low


def lane_nodes():
    lane = iota((8, LANES), 1)
    q = [float(v) for v in cheb_nodes(NODES)]

    def pick(t):
        return jnp.where(t < 2, jnp.where(t == 0, q[0], q[1]), jnp.where(t == 2, q[2], q[3]))

    return pick((lane >> 2) & 3), pick(lane & 3)


def position():
    at = lax.axis_index
    return at("x_hi") * 8 + at("y") * 2 + at("core"), at("z") * 2 + at("x_lo")


def iota(shape, dim):
    return lax.broadcasted_iota(jnp.int32, shape, dim)


PARTS = 8
CHUNKS = (2, 4, 4, 2, 64, LANES)


def pre_kernel(deform, coeffs, out, held, ready, first_cos, first_sin, second_cos, second_sin, sems, out_sems):
    copies = [
        pltpu.make_async_copy(
            coeffs.at[:, 0, pl.ds(2 * p, 2), 0], held.at[:, pl.ds(2 * p, 2)], sems.at[p]
        )
        for p in range(PARTS)
    ]
    sends = [
        pltpu.make_async_copy(
            ready.at[:, :, p & 3, p >> 2], out.at[:, :, p & 3, p >> 2], out_sems.at[p]
        )
        for p in range(PARTS)
    ]
    for copy in copies:
        copy.start()

    nodes = lane_nodes()
    sx, sy = [v.astype(jnp.float32) for v in position()]
    y1, y2 = warp(deform, (nodes[0] + sx) * (1 / 16), (nodes[1] + sy) * (1 / 8))
    y1, y2 = y1[0:1] * 16.0, y2[0:1] * 8.0
    first_cos[...], first_sin[...] = turn(y1 * (iota((16, LANES), 0).astype(jnp.float32) + 0.5))
    second_cos[...], second_sin[...] = turn(y2 * (iota((128, LANES), 0).astype(jnp.float32) + 0.5))
    maps = flip_maps()

    def one(b1):
        c1, s1 = first_cos[b1 : b1 + 1, :], first_sin[b1 : b1 + 1, :]
        for k in range(8):
            turned = []
            for half in range(2):
                at = pl.ds(16 * k + 8 * half, 8)
                c2, s2 = second_cos[at, :], second_sin[at, :]
                c = c1 * c2 - s1 * s2
                s = s1 * c2 + c1 * s2
                re, im = held[0, b1, at, :], held[1, b1, at, :]
                turned.append((re * c + im * s, im * c - re * s))
            for z in range(2):
                low, high = flip(turned[0][z], turned[1][z], maps)
                at = 32 * (k & 1) + 16 * z
                spot = (b1 & 1, k >> 1, (b1 >> 1) & 3, b1 >> 3)
                ready[(*spot, pl.ds(at, 8))] = low
                ready[(*spot, pl.ds(at + 8, 8))] = high

    for q in range(0, PARTS, 2):
        for p in (q, q + 1):
            copies[p].wait()
        for b1 in range(2 * q, 2 * q + 4):
            one(b1)
        for p in (q, q + 1):
            sends[p].start()
    for send in sends:
        send.wait()


def pre(coeffs, deform):
    return pl.pallas_call(
        pre_kernel,
        out_shape=jax.ShapeDtypeStruct(CHUNKS, jnp.float32),
        in_specs=[
            pl.BlockSpec(memory_space=pltpu.SMEM),
            pl.BlockSpec(memory_space=pltpu.HBM),
        ],
        out_specs=pl.BlockSpec(memory_space=pltpu.HBM),
        scratch_shapes=[
            pltpu.VMEM((2, 16, 128, LANES), jnp.float32),
            pltpu.VMEM(CHUNKS, jnp.float32),
            pltpu.VMEM((16, LANES), jnp.float32),
            pltpu.VMEM((16, LANES), jnp.float32),
            pltpu.VMEM((128, LANES), jnp.float32),
            pltpu.VMEM((128, LANES), jnp.float32),
            pltpu.SemaphoreType.DMA((PARTS,)),
            pltpu.SemaphoreType.DMA((PARTS,)),
        ],
        compiler_params=pltpu.CompilerParams(vmem_limit_bytes=60 * MIB),
        cost_estimate=pl.CostEstimate(
            flops=10 * MIB, bytes_accessed=4 * MIB, transcendentals=0
        ),
    )(deform, coeffs)


def phase_rows(tables, deform, store):
    y1, y2 = warp(deform, tables[0], tables[1])
    c, s = turn(tables[2] * y1 + tables[3] * y2)
    real = tables[4] < 0.5
    for child in range(2):
        sine_part = s if child else -s
        store[child, 0] = jnp.where(real, c, sine_part)
        store[child, 1] = jnp.where(real, -sine_part, c)


def dot(a, b):
    return jnp.dot(a, b, precision=lax.Precision.HIGHEST, preferred_element_type=jnp.float32)


def level(pattern, rows, child, part):
    shape = pattern.shape
    real = (iota(shape, 0) & POINTS) == 0
    return pattern * jnp.where(real, rows[child][0][:, part], rows[child][1][:, part])


def build_kernel(
    deform, inner, outer, wide, px, py, px_last, m1_out, m2_out, first, second, rows_in, rows_out, m1, m2, sems
):
    phase_rows(inner, deform, rows_in)
    phase_rows(outer, deform, rows_out)

    def chain(rows, at_x, at_y, at_last, keep):
        last = jnp.concatenate(
            [level(px_last[...], rows, c, slice(at_last, at_last + 64)) for c in range(2)], axis=0
        )
        parts = [dot(last, level(py[...], rows, c, slice(at_y, at_y + 128))) for c in range(2)]
        joined = jnp.concatenate(
            [parts[cy][32 * cx : 32 * cx + keep] for cx in range(2) for cy in range(2)], axis=0
        )
        return [
            dot(joined, level(px[...], rows, c, slice(at_x, at_x + 256))) for c in range(2)
        ]

    def group(g, carry):
        rows = [[rows_in[c, z, pl.ds(g, 1), :] for z in range(2)] for c in range(2)]
        for c, value in enumerate(chain(rows, 0, 256, 384, 16)):
            high, low = split(value)
            m1[g, pl.ds(64 * c, 64), :] = high
            m1[g, pl.ds(128 + 64 * c, 64), :] = low
        return carry

    lax.fori_loop(0, 16, group, 0)
    copies = [
        pltpu.make_async_copy(m1, m1_out, sems.at[0]),
        pltpu.make_async_copy(m2, m2_out, sems.at[1]),
    ]
    copies[0].start()

    rows = [[rows_out[c, z, 0:1, :] for z in range(2)] for c in range(2)]
    for c5, value in enumerate(chain(rows, 512, 768, 896, 32)):
        for c4 in range(2):
            block = dot(value, level(wide[...], rows, c4, slice(0, 512)))
            for c7 in range(2):
                for c6 in range(2):
                    high, low = split(block[64 * c7 + 32 * c6 : 64 * c7 + 32 * c6 + 32])
                    at = 32 * (8 * c5 + 4 * c7 + 2 * c4 + c6)
                    m2[0, pl.ds(at, 32), :] = high
                    m2[1, pl.ds(at, 32), :] = low

    copies[1].start()
    sx, sy = [v.astype(jnp.float32) for v in position()]
    y1, y2 = warp(deform, *lane_nodes())
    c, s = turn(y1[0:1] * (iota((16, LANES), 0).astype(jnp.float32) + (16.0 * sx + 0.5)))
    scale = math.sqrt(0.5) ** 7
    first[0] = c * scale
    first[1] = s * scale
    c, s = turn(y2[0:1] * (iota((128, LANES), 0).astype(jnp.float32) + (128.0 * sy + 0.5)))
    second[0] = c
    second[1] = s
    for copy in copies:
        copy.wait()


def build(deform):
    inner, outer = column_tables()
    consts = [inner, outer, pattern_y_first(), pattern_x(), pattern_y(), pattern_x_last()]
    vmem = pl.BlockSpec(memory_space=pltpu.VMEM)
    return pl.pallas_call(
        build_kernel,
        out_shape=[
            pltpu.HBM((16, 256, 256), jnp.bfloat16),
            pltpu.HBM((2, 512, 512), jnp.bfloat16),
            jax.ShapeDtypeStruct((2, 16, LANES), jnp.float32),
            jax.ShapeDtypeStruct((2, 128, LANES), jnp.float32),
        ],
        in_specs=[pl.BlockSpec(memory_space=pltpu.SMEM)] + [vmem] * 6,
        out_specs=[pl.BlockSpec(memory_space=pltpu.HBM)] * 2 + [vmem] * 2,
        scratch_shapes=[
            pltpu.VMEM((2, 2, 16, 512), jnp.float32),
            pltpu.VMEM((2, 2, 8, 1024), jnp.float32),
            pltpu.VMEM((16, 256, 256), jnp.bfloat16),
            pltpu.VMEM((2, 512, 512), jnp.bfloat16),
            pltpu.SemaphoreType.DMA((2,)),
        ],
        compiler_params=pltpu.CompilerParams(vmem_limit_bytes=16 * MIB),
        cost_estimate=pl.CostEstimate(
            flops=6000 * MIB, bytes_accessed=40 * MIB, transcendentals=0
        ),
    )(deform, *[jnp.asarray(c, dtype=jnp.float32) for c in consts])


def mul(a, b):
    return jnp.dot(a, b, preferred_element_type=jnp.float32)


LOADS = ((0, 4), (4, 16))


def post_kernel(
    m1_in, m2_in, first, second, got, out, m1, m2, x_high, x_low, high, low, acc, done, sems, in_sems
):
    loads = [
        pltpu.make_async_copy(m1_in.at[pl.ds(a, b - a)], m1.at[pl.ds(a, b - a)], in_sems.at[p])
        for p, (a, b) in enumerate(LOADS)
    ] + [pltpu.make_async_copy(m2_in, m2, in_sems.at[2])]
    for load in loads:
        load.start()

    def prepare(g):
        gx, gy = g >> 2, g & 3
        x = [[], []]
        for i in range(4):
            chunk = (i & 1) * 64 + gy * 16 + ((gx & 1) * 2 + (i >> 1)) * 4 + (gx >> 1) * 2
            for j in range(2):
                re, im = got[chunk + j, 0:16, :], got[chunk + j, 16:32, :]
                x[0] += [re, im]
                x[1] += [im, -re]
        x = jnp.concatenate([jnp.concatenate(v, axis=0) for v in x], axis=1)
        x_high[g], x_low[g] = split(x)

    def stage_one(g):
        both = mul(m1[g], x_high[g])
        yh, yl = split(both[:128] + (mul(m1[g, 0:128], x_low[g]) + both[128:]))
        for z in range(2):
            at = pl.ds(32 * g + 16 * z, 16)
            for c13 in range(4):
                for c2 in range(2):
                    rows = slice(32 * c13 + 16 * c2, 32 * c13 + 16 * c2 + 16)
                    lanes = slice(128 * z, 128 * z + 128)
                    high[c13, at, pl.ds(128 * c2, 128)] = yh[rows, lanes]
                    low[c13, at, pl.ds(128 * c2, 128)] = yl[rows, lanes]

    for g in range(16):
        prepare(g)
    for p, (a, b) in enumerate(LOADS):
        loads[p].wait()
        for g in range(a, b):
            stage_one(g)
    loads[2].wait()

    maps = flip_maps()

    def copies(c13):
        return [
            pltpu.make_async_copy(
                done.at[z, pl.ds(4 * c13, 4)], out.at[z, pl.ds(4 * c13, 4)], sems.at[z, c13]
            )
            for z in range(2)
        ]

    for c13 in range(4):

        def finish(c57):
            cx = 4 * c13 + c57
            block = pl.ds(128 * c57, 128)
            acc[block, :] = mul(m2[0, block, :], high[c13]) + (
                mul(m2[0, block, :], low[c13]) + mul(m2[1, block, :], high[c13])
            )
            c1, s1 = first[0, cx : cx + 1, :], first[1, cx : cx + 1, :]
            for cy in range(8):
                at = 128 * c57 + 32 * (cy & 3)
                part = pl.ds(128 * (cy >> 2), 128)
                re, im = [
                    flip(
                        acc[pl.ds(at + 16 * z, 8), part],
                        acc[pl.ds(at + 16 * z + 8, 8), part],
                        maps,
                    )
                    for z in range(2)
                ]
                for half in range(2):
                    rows = pl.ds(64 * half + cy, 8, stride=8)
                    c2, s2 = second[0, rows, :], second[1, rows, :]
                    c, s = c1 * c2 - s1 * s2, s1 * c2 + c1 * s2
                    done[0, cx, rows, :] = re[half] * c - im[half] * s
                    done[1, cx, rows, :] = im[half] * c + re[half] * s

        for c57 in range(4):
            finish(c57)
        for copy in copies(c13):
            copy.start()
    for c13 in range(4):
        for copy in copies(c13):
            copy.wait()


def post(m1, m2, first, second, got):
    vmem = pl.BlockSpec(memory_space=pltpu.VMEM)
    return pl.pallas_call(
        post_kernel,
        out_shape=jax.ShapeDtypeStruct((2, 16, 128, LANES), jnp.float32),
        in_specs=[pl.BlockSpec(memory_space=pltpu.HBM)] * 2 + [vmem] * 3,
        out_specs=pl.BlockSpec(memory_space=pltpu.HBM),
        scratch_shapes=[
            pltpu.VMEM((16, 256, 256), jnp.bfloat16),
            pltpu.VMEM((2, 512, 512), jnp.bfloat16),
            pltpu.VMEM((16, 256, 256), jnp.bfloat16),
            pltpu.VMEM((16, 256, 256), jnp.bfloat16),
            pltpu.VMEM((4, 512, 256), jnp.bfloat16),
            pltpu.VMEM((4, 512, 256), jnp.bfloat16),
            pltpu.VMEM((512, 256), jnp.float32),
            pltpu.VMEM((2, 16, 128, LANES), jnp.float32),
            pltpu.SemaphoreType.DMA((2, 4)),
            pltpu.SemaphoreType.DMA((3,)),
        ],
        compiler_params=pltpu.CompilerParams(vmem_limit_bytes=16 * MIB),
        cost_estimate=pl.CostEstimate(
            flops=4000 * MIB, bytes_accessed=10 * MIB, transcendentals=0
        ),
    )(
        *[pltpu.with_memory_space_constraint(m, pltpu.HBM) for m in (m1, m2)],
        first,
        second,
        got,
    )


def body(coeffs, deform):
    sent = pre(coeffs, deform)
    sent = sent.reshape(128, 32, LANES)
    got = lax.all_to_all(sent, ("core", "z", "y", "x_hi", "x_lo"), 0, 0, tiled=True)
    return post(*build(deform), got)


def solution(mesh):
    fine = Mesh(mesh.devices.reshape(2, 4, 2, 4, 2), ("x_hi", "y", "core", "z", "x_lo"))
    sx, sy = ("x_hi", "y", "core"), ("z", "x_lo")
    return jax.shard_map(
        body,
        mesh=fine,
        in_specs=(P(None, sx, None, sy, None, None), P()),
        out_specs=P(None, sx, sy, None),
        check_vma=False,
    )
```
